128 devices in a mesh: section: 8 (over y, core), dev: 16 (over z, x).
Axes of the slice: x: 4, y: 4, z: 4, core: 2. Of those that a mesh axis runs over, the one named last changes fastest.
Arguments:
- activations: bfloat16 [8, 512, 8192], P('section', None, 'dev'), may hold values from -6 to 6
- q_weight: bfloat16 [8, 8192, 4096], P('section', None, 'dev'), may hold values from -0.125 to 0.125
- out_weight: bfloat16 [8, 4096, 8192], P('section', 'dev'), may hold values from -1 to 1
- kv_weight: bfloat16 [8, 8192, 2048], P('section', 'dev'), may hold values from -0.0625 to 0.0625
- passage_store: bfloat16 [8, 64, 8, 512, 256], P('section', 'dev'), may hold values from -400 to 400
- passage_home: int32 [8, 64], P('section'), may hold values from 0 to 63, as said below
- retrieved: int32 [8, 2, 8], P('section'), may hold values from 0 to 63, as said below
- slot_order: int32 [8, 2, 8], P('section'), may hold values from 0 to 7, each once within a row
- recomputed: int32 [8, 16, 77], P('section'), may hold values from 0 to 511, as said below
- passage_hidden: bfloat16 [8, 16, 77, 8192], P('section', None, None, 'dev'), may hold values from -6 to 6
Outputs:
- passed_on: bfloat16 [8, 512, 8192], P('section', None, 'dev')
The draws below stay inside these ranges and needn't reach their ends.
Inputs may be any that keep to these rules, and one draw needn't show every extreme that they name: `passage_home`: for each section a permutation; rows r * 4 to (r + 1) * 4 - 1 of a section's store lie on device r of dev. The 8 passages of one request differ. In each section, at most 2 of the 16 retrieved entries name passages stored on one device, and some device has exactly 2. `recomputed`: increasing within each slot.
All inputs are finite; a program needn't handle non-finite values.
Results may differ from the reference program's by a relative error of at most 0.035.
The reference program's roundings to bfloat16 on the way count: a program that leaves them out, or rounds other values in their place, can miss the bound.
Values may be sent and summed in bfloat16 or wider, within the bound.
A program may use at most 192 MiB of HBM per device.

```python
import jax
import jax.numpy as jnp
from jax import lax

D = 8192
QH = 32
KVH = 8
HD = 128
PASS_LEN = 512
TOPK = 8
RECOMP = 77
PASS_DEV = 4
REQ_SECTION = 2
QLEN = 256
SLOTS = 16
QROWS = 512
CAP = 2
PASSAGES = 64
N_SECTION = 8
N_DEV = 16


def layout(key):

    def one_section(section_key):
        subkeys = jax.random.split(section_key, 5)
        home_rows = jax.random.permutation(subkeys[0], PASSAGES).astype(jnp.int32)
        row_owner = jnp.argsort(home_rows).astype(jnp.int32)
        lowest = max(1, -((N_DEV - SLOTS) // (CAP - 1)))
        highest = SLOTS // CAP
        doubles = jax.random.randint(subkeys[1], (), lowest, highest + 1)
        tokens_of = jax.random.permutation(subkeys[2], SLOTS).astype(jnp.int32)
        crowded = tokens_of < CAP * doubles
        rank_list = jnp.where(crowded, tokens_of // CAP, doubles + tokens_of - CAP * doubles)
        within = jnp.where(crowded, tokens_of % CAP, 0)
        device_perm = jax.random.permutation(subkeys[3], N_DEV).astype(jnp.int32)
        owners = device_perm[rank_list]
        base_slot = jax.random.randint(subkeys[4], (N_DEV,), 0, PASS_DEV)
        slot_ids = jnp.arange(SLOTS)
        request = slot_ids // TOPK
        clashes = jnp.any((owners[:, None] == owners[None, :]) & (request[:, None] == request[None, :]) & (slot_ids[:, None] != slot_ids[None, :]), axis=1)
        local_slot = (base_slot[owners] + jnp.where(clashes, within, 0)) % PASS_DEV
        chosen = row_owner[owners * PASS_DEV + local_slot]
        return (home_rows, chosen.reshape(REQ_SECTION, TOPK).astype(jnp.int32))
    return jax.vmap(one_section)(jax.random.split(key, N_SECTION))


def draw_passage_home(key, part):
    return layout(key)[0]


def draw_retrieved(key, part):
    return layout(key)[1]


def draw_recomputed(key, part):
    key = jax.random.fold_in(key, 11)
    slot_keys = jax.random.split(key, N_SECTION * SLOTS)

    def pick_rows(slot_key):
        return jnp.sort(jax.random.permutation(slot_key, PASS_LEN)[:RECOMP]).astype(jnp.int32)
    return jax.vmap(pick_rows)(slot_keys).reshape(N_SECTION, SLOTS, RECOMP)


def draw_passage_store(key, part):
    key = jax.random.fold_in(key, 23)
    subkeys = jax.random.split(key, 1)
    full_shape = (N_SECTION, PASSAGES, KVH, PASS_LEN, 2 * HD)
    values = jnp.clip(jax.random.normal(subkeys[0], full_shape, jnp.float32), -6.0, 6.0)
    return values.astype(jnp.bfloat16)


def spiked(result, stream_key, source, target, parts, factor):
    def block_of(dim):
        return (jnp.arange(result.shape[dim]) // (result.shape[dim] // parts)).reshape((-1,) + (1,) * (result.ndim - 1 - dim))

    one_side = jax.random.permutation(stream_key, parts)[block_of(target)]
    far = (block_of(target) + parts // 2) % parts
    return jnp.where((block_of(source) == one_side) | (block_of(source) == far), factor * result, result)


def level_of(key, extent, pieces, low, top_value):
    factor_of = 1.0
    for dim, blocks in pieces:
        draws = jax.random.uniform(jax.random.fold_in(jax.random.fold_in(key, 6), dim), (blocks,), jnp.float32, low / len(pieces), top_value / len(pieces))
        factor_of = factor_of * jnp.repeat(jnp.exp(draws), extent[dim] // blocks).reshape((-1,) + (1,) * (len(extent) - 1 - dim))
    return factor_of


def bell_draw(stream_key, shape, deviation, bound, cuts=(), kind=jnp.bfloat16):
    level = level_of(stream_key, shape, cuts, -0.22, 0.18) if cuts else 1.0
    result = jax.random.normal(stream_key, shape, jnp.float32) * deviation * level
    return jnp.minimum(jnp.maximum(result, -bound), bound).astype(kind)


def heavy_noise(key, shape, width, reach, shards, heavy, kind=jnp.bfloat16):
    drawn = width * jax.random.normal(key, shape, jnp.float32)
    if shards:
        drawn = drawn * level_of(key, shape, shards, -0.22, 0.18)
    return jnp.clip(spiked(drawn, jax.random.fold_in(key, 3), *heavy), -reach, reach).astype(kind)


def setup_inputs(seed: int = 0) -> dict:
    streams_of = jax.random.split(jax.random.key(seed), 11)
    return {
        "activations": bell_draw(streams_of[0], (N_SECTION, QROWS, D), 1.0, 6.0, ((0, 8), (2, 16))),
        "q_weight": bell_draw(streams_of[1], (N_SECTION, D, QH * HD), (D // 4) ** -0.5, 0.125, ((0, 8), (2, 16))),
        "out_weight": heavy_noise(streams_of[2], (N_SECTION, QH * HD, D), (QH * HD // 64) ** -0.5, 1.0, ((0, 8), (1, 16)), (1, 2, 16, 2.0)),
        "kv_weight": bell_draw(streams_of[3], (N_SECTION, D, 2 * KVH * HD), D ** -0.5, 0.0625, ((0, 8), (1, 16))),
        "passage_store": draw_passage_store(jax.random.fold_in(streams_of[10], 71), 0),
        "passage_home": draw_passage_home(jax.random.fold_in(streams_of[10], 71), 0),
        "retrieved": draw_retrieved(jax.random.fold_in(streams_of[10], 71), 0),
        "slot_order": jax.vmap(lambda own: jax.random.permutation(own, TOPK))(jax.random.split(streams_of[7], N_SECTION * REQ_SECTION)).reshape((N_SECTION, REQ_SECTION, TOPK)).astype(jnp.int32),
        "recomputed": draw_recomputed(jax.random.fold_in(streams_of[10], 71), 0),
        "passage_hidden": bell_draw(streams_of[9], (N_SECTION, SLOTS, RECOMP, D), 1.0, 6.0, ((0, 8), (3, 16))),
    }


ROPE_BASE = 500000.0


def rotate(vectors, positions):
    half_dim = HD // 2
    frequency = ROPE_BASE ** (-(jnp.arange(half_dim, dtype=jnp.float32) * (2.0 / HD)))
    angles = positions.astype(jnp.float32)[..., None] * frequency
    cosine = jnp.cos(angles)
    sine_part = jnp.sin(angles)
    first_half = vectors[..., :half_dim]
    second_half = vectors[..., half_dim:]
    return jnp.concatenate([first_half * cosine - second_half * sine_part, second_half * cosine + first_half * sine_part], axis=-1)


def blocked_sum(left, right, blocks):
    block_width = left.shape[1] // blocks

    def add_block(block_index, running):
        piece_cols = lax.dynamic_slice_in_dim(left, block_index * block_width, block_width, 1)
        weight_rows = lax.dynamic_slice_in_dim(right, block_index * block_width, block_width, 0)
        partial_sum = jnp.dot(piece_cols, weight_rows, preferred_element_type=jnp.float32).astype(jnp.bfloat16)
        partial_sum = lax.optimization_barrier(partial_sum)
        return running + partial_sum.astype(jnp.float32)

    initial = jnp.zeros((left.shape[0], right.shape[1]), jnp.float32)
    return lax.fori_loop(0, blocks, add_block, initial)


def blend_slot(block_kv, places, fresh_rows):
    return block_kv.at[:, places, :].set(jnp.swapaxes(fresh_rows, 0, 1))


def section_layer(section_args):
    inputs, q_proj, out_proj, kv_proj, store_rows, home_rows, chosen, order_here, recomp_here, hidden_rows = section_args
    query_rows = inputs.shape[0]
    token_pos = TOPK * PASS_LEN + jnp.arange(QLEN, dtype=jnp.int32)
    queries = jnp.dot(inputs, q_proj, preferred_element_type=jnp.float32).reshape(REQ_SECTION, QLEN, QH, HD)
    queries = rotate(queries, token_pos[None, :, None]).astype(jnp.bfloat16)
    all_rows = jnp.concatenate([inputs, hidden_rows.reshape(SLOTS * RECOMP, D)], axis=0)
    kv_rows = blocked_sum(all_rows, kv_proj, N_DEV).astype(jnp.bfloat16).reshape(-1, KVH, 2 * HD)
    own_rows = kv_rows[:query_rows].reshape(REQ_SECTION, QLEN, KVH, 2 * HD)
    own_keys = rotate(own_rows[..., :HD].astype(jnp.float32), token_pos[None, :, None]).astype(jnp.bfloat16)
    own_values = own_rows[..., HD:]
    fresh_rows = kv_rows[query_rows:].reshape(SLOTS, RECOMP, KVH, 2 * HD)
    offsets = order_here.reshape(SLOTS).astype(jnp.int32) * PASS_LEN
    fresh_pos = offsets[:, None] + recomp_here
    fresh_keys = rotate(fresh_rows[..., :HD].astype(jnp.float32), fresh_pos[:, :, None]).astype(jnp.bfloat16)
    fresh_rows = jnp.concatenate([fresh_keys, fresh_rows[..., HD:]], axis=-1)
    fetched = store_rows[home_rows[chosen.reshape(SLOTS)]]
    moved_keys = rotate(fetched[..., :HD].astype(jnp.float32), offsets[:, None, None]).astype(jnp.bfloat16)
    fetched = jnp.concatenate([moved_keys, fetched[..., HD:]], axis=-1)
    blended = jax.vmap(blend_slot)(fetched, recomp_here, fresh_rows)
    context = blended.reshape(REQ_SECTION, TOPK, KVH, PASS_LEN, 2 * HD).transpose(0, 2, 1, 3, 4)
    context = context.reshape(REQ_SECTION, KVH, TOPK * PASS_LEN, 2 * HD)
    grouped = queries.reshape(REQ_SECTION, QLEN, KVH, QH // KVH, HD).astype(jnp.float32)
    score_scale = HD ** -0.5
    far_scores = jnp.einsum("rqgjd,rgkd->rgjqk", grouped, context[..., :HD].astype(jnp.float32)) * score_scale
    near_scores = jnp.einsum("rqgjd,rkgd->rgjqk", grouped, own_keys.astype(jnp.float32)) * score_scale
    causal = jnp.arange(QLEN)[:, None] >= jnp.arange(QLEN)[None, :]
    near_scores = jnp.where(causal, near_scores, -jnp.inf)
    row_max = jnp.maximum(far_scores.max(axis=-1), near_scores.max(axis=-1))[..., None]
    far_exp = jnp.exp(far_scores - row_max)
    near_exp = jnp.exp(near_scores - row_max)
    denominator = far_exp.sum(axis=-1, keepdims=True) + near_exp.sum(axis=-1, keepdims=True)
    far_weights = (far_exp / denominator).astype(jnp.bfloat16)
    near_weights = (near_exp / denominator).astype(jnp.bfloat16)
    mixed_out = jnp.einsum("rgjqk,rgkd->rqgjd", far_weights.astype(jnp.float32), context[..., HD:].astype(jnp.float32))
    mixed_out = mixed_out + jnp.einsum("rgjqk,rkgd->rqgjd", near_weights.astype(jnp.float32), own_values.astype(jnp.float32))
    attended = mixed_out.astype(jnp.bfloat16).reshape(query_rows, QH * HD)
    return blocked_sum(attended, out_proj, N_DEV).astype(jnp.bfloat16)


def reference(activations, q_weight, out_weight, kv_weight, passage_store, passage_home, retrieved, slot_order, recomputed, passage_hidden):
    branches = lax.map(section_layer, (activations, q_weight, out_weight, kv_weight, passage_store, passage_home, retrieved, slot_order, recomputed, passage_hidden))
    return jnp.roll(branches, 1, axis=0)
```

```python
import functools

import jax
import jax.numpy as jnp
from jax import lax
from jax.experimental import pallas as pl
from jax.experimental.pallas import tpu as pltpu
from jax.sharding import PartitionSpec as P

QH = 32
KVH = 8
HD = 128
PASS_LEN = 512
TOPK = 8
RECOMP = 77
REQ_SECTION = 2
QLEN = 256
SLOTS = 16
CAP = 2
SIDE = 4
N_DEV = 16
PAD = 80
GROUP = QLEN + TOPK * PAD
KEPT = PASS_LEN - RECOMP
HALF = 224
ROPE_BASE = 500000.0
MESH = pl.DeviceIdType.MESH
F32 = jnp.float32
BF16 = jnp.bfloat16
SCALE = HD**-0.5 * 1.4426950408889634


def tables(positions):
    half_dim = HD // 2
    frequency = ROPE_BASE ** (-(jnp.arange(half_dim, dtype=F32) * (2.0 / HD)))
    angles = positions.astype(F32)[..., None] * frequency
    cosine, sine = jnp.cos(angles), jnp.sin(angles)
    return (
        jnp.concatenate([cosine, cosine], axis=-1),
        jnp.concatenate([-sine, sine], axis=-1),
    )


def turned(v, cosine, sine):
    return v * cosine + pltpu.roll(v, HD // 2, axis=1) * sine


def place():
    d = lax.axis_index("dev")
    return lax.axis_index("section"), d // SIDE, lax.rem(d, SIDE)


def around(v, step):
    return lax.rem(v + step + SIDE, SIDE)


def remote(src, dst, send, recv, target):
    return pltpu.make_async_remote_copy(
        src_ref=src,
        dst_ref=dst,
        send_sem=send,
        recv_sem=recv,
        device_id=target,
        device_id_type=MESH,
    )


def pack_kernel(rows, store, keep, cosine, sine, out):
    lanes = lax.broadcasted_iota(jnp.int32, (2 * HALF, PASS_LEN), 1)
    pick = (lanes == keep[0]).astype(F32).astype(BF16)
    for h in range(4):
        kept = jnp.dot(pick, store[0, h], preferred_element_type=F32)
        keys = turned(kept[:, :HD], cosine[0], sine[0]).astype(BF16)
        values = kept[:, HD:].astype(BF16)
        for half in range(2):
            span = slice(half * HALF, (half + 1) * HALF)
            out[h, half, 0, :, :HD] = keys[span]
            out[h, half, 0, :, HD:] = values[span]


def pack(rows, store, keep, cosine, sine):
    out = pl.pallas_call(
        pack_kernel,
        out_shape=jax.ShapeDtypeStruct((KVH, 2, CAP, HALF, 2 * HD), BF16),
        grid_spec=pltpu.PrefetchScalarGridSpec(
            num_scalar_prefetch=1,
            grid=(CAP, 2),
            in_specs=[
                pl.BlockSpec((1, 4, PASS_LEN, 2 * HD), lambda c, g, rows: (rows[c], g, 0, 0)),
                pl.BlockSpec((1, 2 * HALF, 1), lambda c, g, rows: (c, 0, 0)),
                pl.BlockSpec((1, 1, HD), lambda c, g, rows: (c, 0, 0)),
                pl.BlockSpec((1, 1, HD), lambda c, g, rows: (c, 0, 0)),
            ],
            out_specs=pl.BlockSpec(
                (4, 2, 1, HALF, 2 * HD), lambda c, g, rows: (g, 0, c, 0, 0)
            ),
        ),
        compiler_params=pltpu.CompilerParams(vmem_limit_bytes=40 * 2**20),
        name="pack",
    )(rows, store, keep, cosine, sine)
    return out.reshape(N_DEV, CAP, HALF, 2 * HD)


def front_kernel(
    x, hid, kvw, qw, sent, cosq, sinq,
    q_out, kv_out, st_out,
    xall, qv, kvv, hidv, rows, pa, pb, l1, r1, l2, r2, z2, qacc,
    loc, ag_s, ag_r, rs_s, rs_r, st_s, st_r, q_s, q_r,
):
    sec, z, x_ = place()
    me = z * SIDE + x_

    def at(zz, xx):
        return (sec, zz * SIDE + xx)

    right, left = at(z, around(x_, 1)), at(z, around(x_, -1))
    down, up = at(around(z, 1), x_), at(around(z, -1), x_)
    pair = (sec, me + 1 - 2 * lax.rem(me, 2))

    barrier = pltpu.get_barrier_semaphore()
    for k in range(1, N_DEV):
        pl.semaphore_signal(
            barrier, inc=1, device_id=(sec, lax.rem(me + k, N_DEV)), device_id_type=MESH
        )
    loads = [
        pltpu.make_async_copy(kvw, kvv, loc.at[0]),
        pltpu.make_async_copy(hid, hidv, loc.at[1]),
        pltpu.make_async_copy(x.at[pl.ds(0, QLEN)], rows.at[0, pl.ds(0, QLEN)], loc.at[2]),
        pltpu.make_async_copy(x.at[pl.ds(QLEN, QLEN)], rows.at[1, pl.ds(0, QLEN)], loc.at[3]),
        pltpu.make_async_copy(x.at[pl.ds(0, QLEN)], xall.at[0, me], loc.at[4]),
        pltpu.make_async_copy(x.at[pl.ds(QLEN, QLEN)], xall.at[1, me], loc.at[5]),
        pltpu.make_async_copy(qw, qv, loc.at[6]),
        pltpu.make_async_copy(sent.at[me], st_out.at[me], loc.at[7]),
    ]
    for load in loads:
        load.start()
    pl.semaphore_wait(barrier, N_DEV - 1)

    def chunk(half, first, second):
        if half == 0:
            return around(z, second) * SIDE + around(x_, first)
        return around(z, first) * SIDE + around(x_, second)

    ahead = [(right, left), (down, up)]
    top, bottom = pl.ds(0, QLEN // 2), pl.ds(QLEN // 2, QLEN // 2)
    whole = pl.ds(0, QLEN)
    sends = []

    def ag(half, src, span, sem, target, own=False):
        to = xall.at[half, src, span]
        frm = x.at[pl.ds(half * QLEN, QLEN)] if own else to
        copy = remote(frm, to, ag_s.at[sem], ag_r.at[sem], target)
        copy.start()
        sends.append(copy)

    def ag_wait(half, src, span, sem):
        to = xall.at[half, src, span]
        remote(to, to, ag_s.at[sem], ag_r.at[sem], right).wait_recv()

    for half in range(2):
        ag(half, me, whole, 20 * half, ahead[half][0], True)
        ag(half, me, whole, 20 * half + 1, ahead[half][1], True)
    for half in range(2):
        ag(half, me, whole, 20 * half + 4, ahead[1 - half][0], True)
        ag(half, me, whole, 20 * half + 5, ahead[1 - half][1], True)

    for k in (0, 1, 2, 3):
        loads[k].wait()
    for j in range(SLOTS):
        block = rows.at[j // TOPK, pl.ds(QLEN + (j % TOPK) * PAD, PAD)]
        block[...] = jnp.zeros_like(block)
        block[pl.ds(0, RECOMP)] = hidv[j]

    def project(k, carry):
        xx = around(x_, 2 + k // SIDE)
        zz = around(z, 2 + lax.rem(k, SIDE))
        head = 2 * zz + xx // 2
        span = pl.ds(pl.multiple_of(head * 2 * HD, 2 * HD), 2 * HD)
        part = jnp.dot(rows[lax.rem(xx, 2)], kvv[:, span], preferred_element_type=F32)
        part = part.astype(BF16)
        pa[xx, zz] = part[:, :HD]
        pb[zz, xx] = part[:, HD:]
        return carry

    lax.fori_loop(0, N_DEV, project, 0)

    parts = [pa, pb]
    spot = [x_, z]

    def rs(half, src, dst, sem, target):
        copy = remote(src, dst, rs_s.at[sem], rs_r.at[sem], target)
        copy.start()
        sends.append(copy)

    lo, hi = pl.ds(0, 2), pl.ds(2, 2)
    for half in range(2):
        p, c, b = parts[half], spot[half], 9 * half
        rs(half, p.at[around(c, 2), lo], l1.at[half], b, ahead[half][0])
        rs(half, p.at[around(c, 2), hi], r1.at[half], b + 1, ahead[half][1])
        rs(half, p.at[around(c, 1), hi], l2.at[half, hi], b + 2, ahead[half][0])
        rs(half, p.at[around(c, -1), lo], r2.at[half, lo], b + 3, ahead[half][1])

    for half in range(2):
        b = 20 * half
        src = chunk(half, -1, 0)
        ag_wait(half, src, whole, b)
        ag(half, src, top, b + 2, ahead[half][0])
        ag(half, src, whole, b + 8, ahead[1 - half][0])
        ag(half, src, whole, b + 9, ahead[1 - half][1])
        src = chunk(half, 1, 0)
        ag_wait(half, src, whole, b + 1)
        ag(half, src, bottom, b + 3, ahead[half][1])
        ag(half, src, whole, b + 12, ahead[1 - half][0])
        ag(half, src, whole, b + 13, ahead[1 - half][1])
    for half in range(2):
        b = 20 * half
        src = chunk(half, 2, 0)
        ag_wait(half, src, top, b + 2)
        ag_wait(half, src, bottom, b + 3)
        ag(half, src, whole, b + 16, ahead[1 - half][0])
        ag(half, src, whole, b + 17, ahead[1 - half][1])

    def second_axis(k, first):
        for half in range(2):
            b = 20 * half + 4 + 4 * k
            src = chunk(half, first, -1)
            ag_wait(half, src, whole, b)
            ag(half, src, top, b + 2, ahead[1 - half][0])
            src = chunk(half, first, 1)
            ag_wait(half, src, whole, b + 1)
            ag(half, src, bottom, b + 3, ahead[1 - half][1])

    second_axis(0, 0)

    for half in range(2):
        p, c, b = parts[half], spot[half], 9 * half
        remote(l1.at[half], l1.at[half], rs_s.at[b], rs_r.at[b], right).wait_recv()
        for u in range(2):
            block = p.at[around(c, 1), u]
            block[...] = (block[...].astype(F32) + l1[half, u].astype(F32)).astype(BF16)
        rs(half, p.at[around(c, 1), lo], l2.at[half, lo], b + 4, ahead[half][0])
        remote(r1.at[half], r1.at[half], rs_s.at[b + 1], rs_r.at[b + 1], right).wait_recv()
        for u in range(2):
            block = p.at[around(c, -1), 2 + u]
            block[...] = (block[...].astype(F32) + r1[half, u].astype(F32)).astype(BF16)
        rs(half, p.at[around(c, -1), hi], r2.at[half, hi], b + 5, ahead[half][1])

    second_axis(1, -1)
    second_axis(2, 1)
    second_axis(3, 2)

    for k in range(1, N_DEV):
        other = lax.rem(me + k, N_DEV)
        copy = remote(sent.at[other], st_out.at[me], st_s.at[k], st_r.at[k], (sec, other))
        copy.start()
        sends.append(copy)

    for half in range(2):
        p, c, b = parts[half], spot[half], 9 * half
        remote(l2.at[half, hi], l2.at[half, hi], rs_s.at[b + 2], rs_r.at[b + 2], right).wait_recv()
        remote(r2.at[half, lo], r2.at[half, lo], rs_s.at[b + 3], rs_r.at[b + 3], right).wait_recv()
        remote(l2.at[half, lo], l2.at[half, lo], rs_s.at[b + 4], rs_r.at[b + 4], right).wait_recv()
        remote(r2.at[half, hi], r2.at[half, hi], rs_s.at[b + 5], rs_r.at[b + 5], right).wait_recv()
        for u in range(SIDE):
            block = p.at[c, u]
            total = block[...].astype(F32) + l2[half, u].astype(F32) + r2[half, u].astype(F32)
            block[...] = total.astype(BF16)
        for k in range(1, SIDE):
            other = around(spot[1 - half], k)
            target = at(other, x_) if half == 0 else at(z, other)
            rs(half, p.at[c, other], z2.at[half, k - 1], b + 5 + k, target)

    for k in (4, 5, 6):
        loads[k].wait()
    for half in range(2):
        for k in range(SIDE):
            b = 20 * half + 4 + 4 * k
            src = chunk(half, (0, -1, 1, 2)[k], 2)
            ag_wait(half, src, top, b + 2)
            ag_wait(half, src, bottom, b + 3)

    def project_queries(k, carry):
        span = pl.ds(pl.multiple_of(k * 2 * QLEN, 2 * QLEN), 2 * QLEN)
        weight = qv[span, :]
        for half in range(2):
            qacc[half] += jnp.dot(xall[half, k], weight, preferred_element_type=F32)
        return carry

    qacc[...] = jnp.zeros_like(qacc)
    lax.fori_loop(0, N_DEV, project_queries, 0)
    base = 2 * lax.rem(me, 2)
    for half in range(2):
        for j in range(2):
            head = turned(qacc[half, :, j * HD : (j + 1) * HD], cosq[...], sinq[...])
            q_out[half, base + j] = head.astype(BF16)
        block = q_out.at[half, pl.ds(base, 2)]
        copy = remote(block, block, q_s.at[half], q_r.at[half], pair)
        copy.start()
        sends.append(copy)

    for half in range(2):
        p, c, b = parts[half], spot[half], 9 * half
        total = p[c, spot[1 - half]].astype(F32)
        for k in range(1, SIDE):
            block = z2.at[half, k - 1]
            remote(block, block, rs_s.at[b + 5 + k], rs_r.at[b + 5 + k], right).wait_recv()
            total += block[...].astype(F32)
        kv_out[:, half * HD : (half + 1) * HD] = total.astype(BF16)

    for half in range(2):
        block = q_out.at[half, pl.ds(2 - base, 2)]
        remote(block, block, q_s.at[half], q_r.at[half], pair).wait_recv()
    loads[7].wait()
    for k in range(1, N_DEV):
        block = st_out.at[lax.rem(me + N_DEV - k, N_DEV)]
        remote(block, block, st_s.at[k], st_r.at[k], right).wait_recv()
    for copy in sends:
        copy.wait_send()


def front(x, hid, kvw, qw, sent, cosq, sinq):
    anywhere = pl.BlockSpec(memory_space=pl.ANY)
    vmem = pl.BlockSpec(memory_space=pltpu.VMEM)
    dma = pltpu.SemaphoreType.DMA
    d_here = x.shape[1]
    return pl.pallas_call(
        front_kernel,
        out_shape=(
            jax.ShapeDtypeStruct((REQ_SECTION, 4, QLEN, HD), BF16),
            jax.ShapeDtypeStruct((GROUP, 2 * HD), BF16),
            jax.ShapeDtypeStruct((N_DEV, CAP, HALF, 2 * HD), BF16),
        ),
        in_specs=[anywhere] * 5 + [vmem] * 2,
        out_specs=(vmem, vmem, anywhere),
        scratch_shapes=[
            pltpu.VMEM((2, N_DEV, QLEN, d_here), BF16),
            pltpu.VMEM(qw.shape, BF16),
            pltpu.VMEM(kvw.shape, BF16),
            pltpu.VMEM(hid.shape, BF16),
            pltpu.VMEM((REQ_SECTION, GROUP, d_here), BF16),
            pltpu.VMEM((SIDE, SIDE, GROUP, HD), BF16),
            pltpu.VMEM((SIDE, SIDE, GROUP, HD), BF16),
            pltpu.VMEM((2, 2, GROUP, HD), BF16),
            pltpu.VMEM((2, 2, GROUP, HD), BF16),
            pltpu.VMEM((2, SIDE, GROUP, HD), BF16),
            pltpu.VMEM((2, SIDE, GROUP, HD), BF16),
            pltpu.VMEM((2, SIDE - 1, GROUP, HD), BF16),
            pltpu.VMEM((2, QLEN, 2 * HD), F32),
            dma((8,)),
            dma((40,)),
            dma((40,)),
            dma((18,)),
            dma((18,)),
            dma((N_DEV,)),
            dma((N_DEV,)),
            dma((2,)),
            dma((2,)),
        ],
        compiler_params=pltpu.CompilerParams(
            collective_id=0, has_side_effects=True, vmem_limit_bytes=56 * 2**20
        ),
        name="front",
    )(x, hid, kvw, qw, sent, cosq, sinq)


def attend_kernel(entry, mine, q, kv, st, cosk, sink, bias, o, lse, acc, m, l, ks):
    p = mine[0]
    ks[...] = turned(kv[:, :HD].astype(F32), cosk[...], sink[...]).astype(BF16)
    cols = 4 * QLEN

    def step(scores, values):
        old = m[...]
        new = jnp.maximum(old, jnp.max(scores, axis=0, keepdims=True))
        weights = jnp.exp2(scores - new)
        scale = jnp.exp2(old - new)
        m[...] = new
        l[...] = l[...] * scale + jnp.sum(weights, axis=0, keepdims=True)
        acc[...] = acc[...] * scale + lax.dot_general(
            values, weights.astype(BF16), (((0,), (0,)), ((), ())), preferred_element_type=F32
        )

    def score(keys, queries):
        s = lax.dot_general(
            keys, queries, (((1,), (1,)), ((), ())), preferred_element_type=F32
        )
        return s * SCALE

    for r in range(REQ_SECTION):
        m[...] = jnp.full_like(m, -1e30)
        l[...] = jnp.zeros_like(l)
        acc[...] = jnp.zeros_like(acc)
        queries = q[r].reshape(cols, HD)
        for k in range(TOPK):
            e = entry[r * TOPK + k]
            block = st.at[e]
            s = score(block[:, :HD], queries) + bias[pl.ds(0, HALF)]
            step(s, block[:, HD:])

        @pl.when(p == r)
        def _():
            for k in range(TOPK // 2):
                span = pl.ds(QLEN + 2 * k * PAD, 2 * PAD)
                s = score(ks[span, :], queries) + bias[pl.ds(HALF, 2 * PAD)]
                step(s, kv[span, HD:])
            s = score(ks[pl.ds(0, QLEN), :], queries)
            keys_at = lax.broadcasted_iota(jnp.int32, (QLEN, cols), 0)
            query_at = lax.rem(lax.broadcasted_iota(jnp.int32, (QLEN, cols), 1), QLEN)
            s = jnp.where(keys_at <= query_at, s, -jnp.inf)
            step(s, kv[pl.ds(0, QLEN), HD:])

        done = (acc[...] / l[...]).astype(BF16)
        level = m[...] + jnp.log2(l[...])
        for j in range(4):
            span = slice(j * QLEN, (j + 1) * QLEN)
            here = pl.ds(r * QLEN, QLEN)
            o[j // 2, pl.ds((j % 2) * HD, HD), here] = done[:, span]
            lse[j // 2, pl.ds(j % 2, 1), here] = level[:, span]


def attend(entry, mine, q, kv, st, cosk, sink, bias):
    vmem = pl.BlockSpec(memory_space=pltpu.VMEM)
    smem = pl.BlockSpec(memory_space=pltpu.SMEM)
    return pl.pallas_call(
        attend_kernel,
        out_shape=(
            jax.ShapeDtypeStruct((2, 2 * HD, REQ_SECTION * QLEN), BF16),
            jax.ShapeDtypeStruct((2, 8, REQ_SECTION * QLEN), F32),
        ),
        in_specs=[smem, smem] + [vmem] * 6,
        out_specs=(vmem, vmem),
        scratch_shapes=[
            pltpu.VMEM((HD, 4 * QLEN), F32),
            pltpu.VMEM((1, 4 * QLEN), F32),
            pltpu.VMEM((1, 4 * QLEN), F32),
            pltpu.VMEM((GROUP, HD), BF16),
        ],
        compiler_params=pltpu.CompilerParams(vmem_limit_bytes=48 * 2**20),
        name="attend",
    )(entry, mine, q, kv, st, cosk, sink, bias)


BLOCKS = 2


def back_kernel(
    o, lse, ow, out,
    wv, other_o, other_lse, att, pa, pb, l1, r1, l2, r2, z2,
    loc, ex_s, ex_r, rs_s, rs_r,
):
    sec, z, x_ = place()
    me = z * SIDE + x_
    sections = lax.axis_size("section")
    after, before = lax.rem(sec + 1, sections), lax.rem(sec + sections - 1, sections)
    mine = lax.rem(me, 2)

    def at(zz, xx):
        return (sec, zz * SIDE + xx)

    right, left = at(z, around(x_, 1)), at(z, around(x_, -1))
    down, up = at(around(z, 1), x_), at(around(z, -1), x_)
    pair = (sec, me + 1 - 2 * mine)
    barrier = pltpu.get_barrier_semaphore()
    greeted = [right, left, down, up]
    for s in (after, before):
        greeted.append((s, me))
        for k in range(1, SIDE):
            greeted.append((s, z * SIDE + around(x_, k)))
            greeted.append((s, around(z, k) * SIDE + x_))
    for target in greeted:
        pl.semaphore_signal(barrier, inc=1, device_id=target, device_id_type=MESH)
    load = pltpu.make_async_copy(ow, wv, loc.at[0])
    load.start()
    pl.semaphore_wait(barrier, len(greeted))
    sends = []

    def push(src, dst, send, recv, target):
        copy = remote(src, dst, send, recv, target)
        copy.start()
        sends.append(copy)

    push(o.at[1 - mine], other_o, ex_s.at[0], ex_r.at[0], pair)
    push(lse.at[1 - mine], other_lse, ex_s.at[1], ex_r.at[1], pair)
    remote(other_o, other_o, ex_s.at[0], ex_r.at[0], pair).wait_recv()
    remote(other_lse, other_lse, ex_s.at[1], ex_r.at[1], pair).wait_recv()
    for j in range(2):
        a, b = lse[mine, pl.ds(j, 1), :], other_lse[pl.ds(j, 1), :]
        most = jnp.maximum(a, b)
        a, b = jnp.exp2(a - most), jnp.exp2(b - most)
        span = pl.ds(j * HD, HD)
        joined = o[mine, span, :].astype(F32) * a + other_o[span, :].astype(F32) * b
        joined = joined / (a + b)
        att[:, j * HD : (j + 1) * HD] = joined.T.astype(BF16)
    load.wait()

    ahead = [(right, left), (down, up)]
    spot = [x_, z]
    parts = [pa, pb]
    lo, hi = pl.ds(0, 2), pl.ds(2, 2)
    size = REQ_SECTION * QLEN // BLOCKS
    part = size // 2

    def compute(b):
        def one(k, carry):
            xx = around(x_, 2 + k // SIDE)
            zz = around(z, 2 + lax.rem(k, SIDE))
            span = pl.ds(pl.multiple_of((zz * SIDE + xx) * 512, 512), 512)
            got = jnp.dot(
                att[b * size : (b + 1) * size, :], wv[:, span], preferred_element_type=F32
            ).astype(BF16)
            pa[b, xx, zz] = got[:part]
            pb[b, zz, xx] = got[part:]
            return carry

        lax.fori_loop(0, N_DEV, one, 0)

    def first(b):
        for half in range(2):
            p, c, s = parts[half], spot[half], 20 * b + 10 * half
            push(p.at[b, around(c, 2), lo], l1.at[b, half], rs_s.at[s], rs_r.at[s], ahead[half][0])
            push(p.at[b, around(c, 2), hi], r1.at[b, half], rs_s.at[s + 1], rs_r.at[s + 1], ahead[half][1])
            push(p.at[b, around(c, 1), hi], l2.at[b, half, hi], rs_s.at[s + 2], rs_r.at[s + 2], ahead[half][0])
            push(p.at[b, around(c, -1), lo], r2.at[b, half, lo], rs_s.at[s + 3], rs_r.at[s + 3], ahead[half][1])

    def arrived(block, s):
        remote(block, block, rs_s.at[s], rs_r.at[s], right).wait_recv()

    def second(b):
        for half in range(2):
            p, c, s = parts[half], spot[half], 20 * b + 10 * half
            arrived(l1.at[b, half], s)
            for u in range(2):
                block = p.at[b, around(c, 1), u]
                block[...] = (block[...].astype(F32) + l1[b, half, u].astype(F32)).astype(BF16)
            push(p.at[b, around(c, 1), lo], l2.at[b, half, lo], rs_s.at[s + 4], rs_r.at[s + 4], ahead[half][0])
            arrived(r1.at[b, half], s + 1)
            for u in range(2):
                block = p.at[b, around(c, -1), 2 + u]
                block[...] = (block[...].astype(F32) + r1[b, half, u].astype(F32)).astype(BF16)
            push(p.at[b, around(c, -1), hi], r2.at[b, half, hi], rs_s.at[s + 5], rs_r.at[s + 5], ahead[half][1])

    def third(b):
        for half in range(2):
            p, c, s = parts[half], spot[half], 20 * b + 10 * half
            arrived(l2.at[b, half, hi], s + 2)
            arrived(r2.at[b, half, lo], s + 3)
            arrived(l2.at[b, half, lo], s + 4)
            arrived(r2.at[b, half, hi], s + 5)
            for u in range(SIDE):
                block = p.at[b, c, u]
                total = block[...].astype(F32) + l2[b, half, u].astype(F32)
                block[...] = (total + r2[b, half, u].astype(F32)).astype(BF16)
            for k in range(SIDE):
                other = around(spot[1 - half], k)
                target = (after, other * SIDE + x_) if half == 0 else (after, z * SIDE + other)
                push(p.at[b, c, other], z2.at[b, half, k], rs_s.at[s + 6 + k], rs_r.at[s + 6 + k], target)

    def fourth(b):
        for half in range(2):
            s = 20 * b + 10 * half
            total = None
            for k in range(SIDE):
                arrived(z2.at[b, half, k], s + 6 + k)
                block = z2[b, half, k].astype(F32)
                total = block if total is None else total + block
            out[pl.ds(b * size + half * part, part), :] = total.astype(BF16)

    compute(0)
    first(0)
    for b in range(BLOCKS):
        if b + 1 < BLOCKS:
            compute(b + 1)
            first(b + 1)
        second(b)
        if b > 0:
            third(b - 1)
    third(BLOCKS - 1)
    for b in range(BLOCKS):
        fourth(b)
    for copy in sends:
        copy.wait_send()


def back(o, lse, ow):
    vmem = pl.BlockSpec(memory_space=pltpu.VMEM)
    dma = pltpu.SemaphoreType.DMA
    rows = REQ_SECTION * QLEN
    part = rows // BLOCKS // 2
    width = ow.shape[1] // N_DEV
    return pl.pallas_call(
        back_kernel,
        out_shape=jax.ShapeDtypeStruct((rows, width), BF16),
        in_specs=[vmem, vmem, pl.BlockSpec(memory_space=pl.ANY)],
        out_specs=vmem,
        scratch_shapes=[
            pltpu.VMEM(ow.shape, BF16),
            pltpu.VMEM(o.shape[1:], BF16),
            pltpu.VMEM(lse.shape[1:], F32),
            pltpu.VMEM((rows, 2 * HD), BF16),
            pltpu.VMEM((BLOCKS, SIDE, SIDE, part, width), BF16),
            pltpu.VMEM((BLOCKS, SIDE, SIDE, part, width), BF16),
            pltpu.VMEM((BLOCKS, 2, 2, part, width), BF16),
            pltpu.VMEM((BLOCKS, 2, 2, part, width), BF16),
            pltpu.VMEM((BLOCKS, 2, SIDE, part, width), BF16),
            pltpu.VMEM((BLOCKS, 2, SIDE, part, width), BF16),
            pltpu.VMEM((BLOCKS, 2, SIDE, part, width), BF16),
            dma((1,)),
            dma((2,)),
            dma((2,)),
            dma((20 * BLOCKS,)),
            dma((20 * BLOCKS,)),
        ],
        compiler_params=pltpu.CompilerParams(
            collective_id=1, has_side_effects=True, vmem_limit_bytes=56 * 2**20
        ),
        name="back",
    )(o, lse, ow)


def body(
    activations, q_weight, out_weight, kv_weight, passage_store,
    passage_home, retrieved, slot_order, recomputed, passage_hidden,
):
    me = lax.axis_index("dev")
    per_device = passage_store.shape[1]
    home = passage_home[0][retrieved[0].reshape(SLOTS)]
    owners, store_slot = home // per_device, home % per_device
    offsets = slot_order[0].reshape(SLOTS) * PASS_LEN
    recomp = recomputed[0]
    earlier = jnp.arange(SLOTS)[None, :] < jnp.arange(SLOTS)[:, None]
    rank = jnp.sum(earlier & (owners[None, :] == owners[:, None]), axis=1)
    entry = (owners * CAP + rank).astype(jnp.int32)
    chosen = entry[None, :] == (me * CAP + jnp.arange(CAP))[:, None]

    def choose(values):
        shape = chosen.shape + (1,) * (values.ndim - 1)
        return jnp.sum(jnp.where(chosen.reshape(shape), values[None], 0), axis=1)

    rows = choose(store_slot).astype(jnp.int32)
    cos_s, sin_s = tables(choose(offsets))
    dropped = choose(recomp)
    index = jnp.arange(2 * HALF, dtype=jnp.int32)
    before = dropped - jnp.arange(RECOMP, dtype=jnp.int32)
    keep = index[None] + jnp.sum(before[:, :, None] <= index[None, None], axis=1)
    keep = keep.astype(jnp.int32)[:, :, None]
    sent = pack(rows, passage_store[0], keep, cos_s[:, None], sin_s[:, None])

    token_pos = TOPK * PASS_LEN + jnp.arange(QLEN, dtype=jnp.int32)
    cosq, sinq = tables(token_pos)
    q, kv, st = front(
        activations[0], passage_hidden[0], kv_weight[0], q_weight[0], sent, cosq, sinq
    )
    mine = lax.rem(me, 2).astype(jnp.int32)
    fresh_pos = jnp.pad(offsets[:, None] + recomp, ((0, 0), (0, PAD - RECOMP)))
    fresh_pos = jnp.where(mine == 0, fresh_pos[:TOPK], fresh_pos[TOPK:]).reshape(-1)
    cosk, sink = tables(jnp.concatenate([token_pos, fresh_pos]))
    valid = jnp.concatenate(
        [
            jnp.arange(HALF) < jnp.where(mine == 0, HALF, KEPT - HALF),
            jnp.arange(2 * PAD) % PAD < RECOMP,
        ]
    )
    bias = jnp.where(valid, 0.0, -jnp.inf).astype(F32)[:, None]
    o, lse = attend(
        entry, mine[None], q, kv, st.reshape(N_DEV * CAP, HALF, 2 * HD), cosk, sink, bias
    )
    return back(o, lse, out_weight[0])[None]


def solution(mesh):
    in_specs = (
        P("section", None, "dev"),
        P("section", None, "dev"),
        P("section", "dev", None),
        P("section", "dev", None),
        P("section", "dev", None, None, None),
        P("section", None),
        P("section", None, None),
        P("section", None, None),
        P("section", None, None),
        P("section", None, None, "dev"),
    )
    out_specs = P("section", None, "dev")
    return jax.shard_map(body, mesh=mesh, in_specs=in_specs, out_specs=out_specs, check_vma=False)
```

```python
import functools

import jax
import jax.numpy as jnp
from jax import lax
from jax.experimental import pallas as pl
from jax.experimental.pallas import tpu as pltpu
from jax.sharding import PartitionSpec as P

QH = 32
KVH = 8
HD = 128
PASS_LEN = 512
TOPK = 8
RECOMP = 77
REQ_SECTION = 2
QLEN = 256
SLOTS = 16
CAP = 2
PASS_DEV = 4
SIDE = 4
N_DEV = 16
FRESH = 39
GROUP = QLEN + FRESH * SLOTS
FROWS = 320
KEPT = PASS_LEN - RECOMP
HALF = 224
PIECE = HALF // 2
BLOCKS = 4
ROPE_BASE = 500000.0
MESH = pl.DeviceIdType.MESH
F32 = jnp.float32
BF16 = jnp.bfloat16
SCALE = HD**-0.5 * 1.4426950408889634


def lane_tables(frequency, positions):
    angles = positions * frequency
    sign = jnp.where(lax.broadcasted_iota(jnp.int32, (1, HD), 1) < HD // 2, -1.0, 1.0)
    return jnp.cos(angles), jnp.sin(angles) * sign


def turned(v, cosine, sine):
    return v * cosine + pltpu.roll(v, HD // 2, axis=1) * sine


def place():
    d = lax.axis_index("dev")
    return lax.axis_index("section"), d // SIDE, lax.rem(d, SIDE)


def around(v, step):
    return lax.rem(v + step + SIDE, SIDE)


def remote(src, dst, send, recv, target):
    return pltpu.make_async_remote_copy(
        src_ref=src,
        dst_ref=dst,
        send_sem=send,
        recv_sem=recv,
        device_id=target,
        device_id_type=MESH,
    )


STEPS = (
    (0, 1), (0, 3), (1, 0), (3, 0), (1, 1), (3, 3), (1, 3), (3, 1),
    (0, 2), (2, 0), (2, 1), (2, 3), (1, 2), (3, 2), (2, 2),
)


def layer_kernel(
    home, retrieved, order, x, hid, kvw, qw, ow, store, rec, freq, pos, out,
    ent, xall, qv, kvv, rows, pa, pb, l1, r1, l2, r2, z2, qacc,
    storev, sent, st0, st1, q4, kf, vf, ko, vo, acc, m, l,
    oall, lall, oin, lin, wv, att, bl1, br1, bl2, br2, bz2, outv,
    loc, own_s, ag_s, ag_r, rs_s, rs_r, st_s, st_r, q_s, q_r, ex_s, ex_r, br_s, br_r,
):
    sec = lax.axis_index("section")
    me = lax.axis_index("dev")
    z, x_ = me // SIDE, lax.rem(me, SIDE)
    sections = lax.axis_size("section")
    after, before = lax.rem(sec + 1, sections), lax.rem(sec + sections - 1, sections)
    mine = lax.rem(me, 2)

    def at(zz, xx):
        return (sec, zz * SIDE + xx)

    right, left = at(z, around(x_, 1)), at(z, around(x_, -1))
    down, up = at(around(z, 1), x_), at(around(z, -1), x_)
    pair = (sec, me + 1 - 2 * mine)
    ahead = [(right, left), (down, up)]
    spot = [x_, z]

    greeted = [(sec, lax.rem(me + k, N_DEV)) for k in range(1, N_DEV)]
    for s in (after, before):
        greeted.append((s, me))
        for k in range(1, SIDE):
            greeted.append((s, z * SIDE + around(x_, k)))
            greeted.append((s, around(z, k) * SIDE + x_))
    barrier = pltpu.get_barrier_semaphore()
    for target in greeted:
        pl.semaphore_signal(barrier, inc=1, device_id=target, device_id_type=MESH)

    first_rows, last_rows = FRESH * SLOTS, (RECOMP - FRESH) * SLOTS
    loads = [
        pltpu.make_async_copy(kvw, kvv, loc.at[0]),
        pltpu.make_async_copy(x.at[pl.ds(0, QLEN)], rows.at[0, pl.ds(0, QLEN)], loc.at[1]),
        pltpu.make_async_copy(x.at[pl.ds(QLEN, QLEN)], rows.at[1, pl.ds(0, QLEN)], loc.at[2]),
        pltpu.make_async_copy(
            hid.at[pl.ds(0, first_rows)], rows.at[0, pl.ds(QLEN, first_rows)], loc.at[3]
        ),
        pltpu.make_async_copy(
            hid.at[pl.ds(first_rows, last_rows)], rows.at[1, pl.ds(QLEN, last_rows)], loc.at[4]
        ),
        pltpu.make_async_copy(store, storev, loc.at[5]),
        pltpu.make_async_copy(qw, qv, loc.at[6]),
        pltpu.make_async_copy(x.at[pl.ds(0, QLEN)], xall.at[0, me], loc.at[7]),
        pltpu.make_async_copy(x.at[pl.ds(QLEN, QLEN)], xall.at[1, me], loc.at[8]),
        pltpu.make_async_copy(ow, wv, loc.at[9]),
    ]
    for load in loads:
        load.start()
    rest = rows.at[1, pl.ds(QLEN + last_rows, GROUP - QLEN - last_rows)]
    rest[...] = jnp.zeros_like(rest)
    pl.semaphore_wait(barrier, len(greeted))

    def chunk(half, first, second):
        if half == 0:
            return around(z, second) * SIDE + around(x_, first)
        return around(z, first) * SIDE + around(x_, second)

    top, bottom = pl.ds(0, QLEN // 2), pl.ds(QLEN // 2, QLEN // 2)
    whole = pl.ds(0, QLEN)
    ag_sends, sends = [], []

    def ag(half, src, span, sem, target, own=False):
        to = xall.at[half, src, span]
        frm = x.at[pl.ds(half * QLEN, QLEN)] if own else to
        copy = remote(frm, to, ag_s.at[sem], ag_r.at[sem], target)
        copy.start()
        ag_sends.append(copy)

    def ag_wait(half, src, span, sem):
        to = xall.at[half, src, span]
        remote(to, to, ag_s.at[sem], ag_r.at[sem], right).wait_recv()

    for half in range(2):
        ag(half, me, whole, 20 * half, ahead[half][0], True)
        ag(half, me, whole, 20 * half + 1, ahead[half][1], True)
    for half in range(2):
        ag(half, me, whole, 20 * half + 4, ahead[1 - half][0], True)
        ag(half, me, whole, 20 * half + 5, ahead[1 - half][1], True)

    def push(group, src, dst, send, recv, target):
        copy = remote(src, dst, send, recv, target)
        copy.start()
        group.append(copy)

    def arrived(block, send, recv):
        remote(block, block, send, recv, right).wait_recv()

    def project(xx, zz):
        head = 2 * zz + xx // 2
        span = pl.ds(pl.multiple_of(head * 2 * HD, 2 * HD), 2 * HD)
        part = jnp.dot(rows[lax.rem(xx, 2)], kvv[:, span], preferred_element_type=F32)
        part = part.astype(BF16)
        pa[xx, zz] = part[:, :HD]
        pb[zz, xx] = part[:, HD:]

    def loop(count, step):
        def one(k, carry):
            step(k)
            return carry

        lax.fori_loop(0, count, one, 0)

    def skip_two(t):
        return t + t // 2

    parts = [pa, pb]
    lo, hi = pl.ds(0, 2), pl.ds(2, 2)

    def rs(half, src, dst, sem, target):
        push(sends, src, dst, rs_s.at[sem], rs_r.at[sem], target)

    def rs_first(half):
        p, c, b = parts[half], spot[half], 9 * half
        rs(half, p.at[around(c, 2), lo], l1.at[half], b, ahead[half][0])
        rs(half, p.at[around(c, 2), hi], r1.at[half], b + 1, ahead[half][1])

    for k in range(5):
        loads[k].wait()
    loop(SIDE, lambda k: project(around(x_, 2), around(z, k)))
    rs_first(0)
    loop(SIDE - 1, lambda k: project(around(x_, skip_two(k)), around(z, 2)))
    rs_first(1)
    loop(9, lambda k: project(around(x_, skip_two(k // 3)), around(z, skip_two(lax.rem(k, 3)))))
    for half in range(2):
        p, c, b = parts[half], spot[half], 9 * half
        rs(half, p.at[around(c, 1), hi], l2.at[half, hi], b + 2, ahead[half][0])
        rs(half, p.at[around(c, -1), lo], r2.at[half, lo], b + 3, ahead[half][1])

    for half in range(2):
        b = 20 * half
        src = chunk(half, -1, 0)
        ag_wait(half, src, whole, b)
        ag(half, src, top, b + 2, ahead[half][0])
        ag(half, src, whole, b + 8, ahead[1 - half][0])
        ag(half, src, whole, b + 9, ahead[1 - half][1])
        src = chunk(half, 1, 0)
        ag_wait(half, src, whole, b + 1)
        ag(half, src, bottom, b + 3, ahead[half][1])
        ag(half, src, whole, b + 12, ahead[1 - half][0])
        ag(half, src, whole, b + 13, ahead[1 - half][1])

    homes = [home[0, retrieved[0, j // TOPK, j % TOPK]] for j in range(SLOTS)]
    owners = [h // PASS_DEV for h in homes]
    entries = []
    for j in range(SLOTS):
        rank = jnp.int32(0)
        for i in range(j):
            rank = rank + jnp.where(owners[i] == owners[j], 1, 0)
        entries.append(owners[j] * CAP + rank)
        ent[j] = entries[j]
    frequency = freq[...]
    loads[5].wait()
    for c in range(CAP):
        row, slot, offset = jnp.int32(0), jnp.int32(0), jnp.int32(0)
        for j in range(SLOTS):
            hit = entries[j] == me * CAP + c
            row = jnp.where(hit, lax.rem(homes[j], PASS_DEV), row)
            slot = jnp.where(hit, j, slot)
            offset = jnp.where(hit, order[0, j // TOPK, j % TOPK] * PASS_LEN, offset)
        dropped = rec[0, pl.ds(slot, 1), :]
        ahead_of = (dropped - lax.broadcasted_iota(jnp.int32, (1, RECOMP), 1)).astype(F32)
        index = lax.broadcasted_iota(jnp.int32, (2 * HALF, RECOMP), 0).astype(F32)
        count = jnp.sum(jnp.where(ahead_of <= index, 1.0, 0.0), axis=1, keepdims=True)
        keep = index[:, :1] + count
        lanes = lax.broadcasted_iota(jnp.int32, (2 * HALF, PASS_LEN), 1).astype(F32)
        pick = jnp.where(lanes == keep, 1.0, 0.0).astype(BF16)
        cosine, sine = lane_tables(frequency, offset.astype(F32))

        def one_head(h):
            kept = jnp.dot(pick, storev[row, h], preferred_element_type=F32)
            keys = turned(kept[:, :HD], cosine, sine).astype(BF16)
            values = kept[:, HD:].astype(BF16)
            for half in range(2):
                for g in range(2):
                    start = half * HALF + g * PIECE
                    to = sent.at[g, 2 * h + half, c]
                    to[:, :HD] = keys[start : start + PIECE]
                    to[:, HD:] = values[start : start + PIECE]

        loop(KVH, one_head)

    st = [st0, st1]
    for g in range(2):
        copy = pltpu.make_async_copy(
            sent.at[g, me], st[g].at[pl.ds(2 * me, CAP)], own_s.at[g]
        )
        copy.start()

    def passages(g):
        for k, (dz, dx) in enumerate(STEPS):
            other = around(z, dz) * SIDE + around(x_, dx)
            sem = len(STEPS) * g + k
            push(sends, sent.at[g, other], st[g].at[pl.ds(2 * me, CAP)],
                 st_s.at[sem], st_r.at[sem], (sec, other))

    def passages_wait(g):
        pltpu.make_async_copy(
            sent.at[g, me], st[g].at[pl.ds(2 * me, CAP)], own_s.at[g]
        ).wait()
        for k, (dz, dx) in enumerate(STEPS):
            other = around(z, -dz) * SIDE + around(x_, -dx)
            sem = len(STEPS) * g + k
            arrived(st[g].at[pl.ds(2 * other, CAP)], st_s.at[sem], st_r.at[sem])

    for half in range(2):
        b = 20 * half
        src = chunk(half, 2, 0)
        ag_wait(half, src, top, b + 2)
        ag_wait(half, src, bottom, b + 3)
        ag(half, src, whole, b + 16, ahead[1 - half][0])
        ag(half, src, whole, b + 17, ahead[1 - half][1])

    def second_axis(k, first):
        for half in range(2):
            b = 20 * half + 4 + 4 * k
            src = chunk(half, first, -1)
            ag_wait(half, src, whole, b)
            ag(half, src, top, b + 2, ahead[1 - half][0])
            src = chunk(half, first, 1)
            ag_wait(half, src, whole, b + 1)
            ag(half, src, bottom, b + 3, ahead[1 - half][1])

    second_axis(0, 0)

    for half in range(2):
        p, c, b = parts[half], spot[half], 9 * half
        arrived(l1.at[half], rs_s.at[b], rs_r.at[b])
        for u in range(2):
            block = p.at[around(c, 1), u]
            block[...] = (block[...].astype(F32) + l1[half, u].astype(F32)).astype(BF16)
        rs(half, p.at[around(c, 1), lo], l2.at[half, lo], b + 4, ahead[half][0])
        arrived(r1.at[half], rs_s.at[b + 1], rs_r.at[b + 1])
        for u in range(2):
            block = p.at[around(c, -1), 2 + u]
            block[...] = (block[...].astype(F32) + r1[half, u].astype(F32)).astype(BF16)
        rs(half, p.at[around(c, -1), hi], r2.at[half, hi], b + 5, ahead[half][1])

    second_axis(1, -1)
    second_axis(2, 1)
    passages(0)
    second_axis(3, 2)

    for half in range(2):
        p, c, b = parts[half], spot[half], 9 * half
        arrived(l2.at[half, hi], rs_s.at[b + 2], rs_r.at[b + 2])
        arrived(r2.at[half, lo], rs_s.at[b + 3], rs_r.at[b + 3])
        arrived(l2.at[half, lo], rs_s.at[b + 4], rs_r.at[b + 4])
        arrived(r2.at[half, hi], rs_s.at[b + 5], rs_r.at[b + 5])
        for u in range(SIDE):
            block = p.at[c, u]
            total = block[...].astype(F32) + l2[half, u].astype(F32) + r2[half, u].astype(F32)
            block[...] = total.astype(BF16)
        for k in (1, 3, 2):
            other = around(spot[1 - half], k)
            target = at(other, x_) if half == 0 else at(z, other)
            rs(half, p.at[c, other], z2.at[half, k - 1], b + 5 + k, target)
    passages(1)

    for k in (6, 7, 8):
        loads[k].wait()
    for half in range(2):
        for k in range(SIDE):
            b = 20 * half + 4 + 4 * k
            src = chunk(half, (0, -1, 1, 2)[k], 2)
            ag_wait(half, src, top, b + 2)
            ag_wait(half, src, bottom, b + 3)

    def project_queries(k):
        span = pl.ds(pl.multiple_of(k * 2 * QLEN, 2 * QLEN), 2 * QLEN)
        weight = qv[span, :]
        for half in range(2):
            qacc[half] += jnp.dot(xall[half, k], weight, preferred_element_type=F32)

    qacc[...] = jnp.zeros_like(qacc)
    loop(N_DEV, project_queries)
    token_at = lax.broadcasted_iota(jnp.int32, (QLEN, 1), 0) + TOPK * PASS_LEN
    cosine, sine = lane_tables(frequency, token_at.astype(F32))
    base = 2 * mine
    for half in range(2):
        for j in range(2):
            head = turned(qacc[half, :, j * HD : (j + 1) * HD], cosine, sine)
            q4[half, base + j] = head.astype(BF16)
        block = q4.at[half, pl.ds(base, 2)]
        push(sends, block, block, q_s.at[half], q_r.at[half], pair)

    cosine, sine = lane_tables(frequency, pos[...])
    for half in range(2):
        p, c, b = parts[half], spot[half], 9 * half
        total = p[c, spot[1 - half]].astype(F32)
        for k in range(1, SIDE):
            block = z2.at[half, k - 1]
            arrived(block, rs_s.at[b + 5 + k], rs_r.at[b + 5 + k])
            total += block[...].astype(F32)
        total = total.astype(BF16).astype(F32)
        if half == 0:
            total = turned(total, cosine, sine)
        own_to, fresh_to = (ko, kf) if half == 0 else (vo, vf)
        own_to[...] = total[:QLEN].astype(BF16)
        fresh = total[QLEN:].reshape(FRESH, SLOTS, HD)
        for r in range(REQ_SECTION):
            rows_of = fresh[:, r * TOPK : (r + 1) * TOPK].reshape(FRESH * TOPK, HD)
            filler = jnp.zeros((FROWS - FRESH * TOPK, HD), F32)
            fresh_to[r] = jnp.concatenate([rows_of, filler], axis=0).astype(BF16)

    cols = 4 * QLEN

    def score(keys, queries):
        s = lax.dot_general(
            keys, queries, (((1,), (1,)), ((), ())), preferred_element_type=F32
        )
        return s * SCALE

    def update(r, scores, values):
        old = m[r]
        new = old
        for s in scores:
            new = jnp.maximum(new, jnp.max(s, axis=0, keepdims=True))
        scale = jnp.exp2(old - new)
        total, mixed = l[r] * scale, acc[r] * scale
        for s, v in zip(scores, values):
            weights = jnp.exp2(s - new)
            total = total + jnp.sum(weights, axis=0, keepdims=True)
            mixed = mixed + lax.dot_general(
                v, weights.astype(BF16), (((0,), (0,)), ((), ())), preferred_element_type=F32
            )
        m[r], l[r], acc[r] = new, total, mixed

    def bias(count, valid):
        index = lax.broadcasted_iota(jnp.int32, (count, 1), 0)
        return jnp.where(index < valid, 0.0, -jnp.inf)

    def queries_of(r):
        return q4[r].reshape(cols, HD)

    def stored(r, g):
        def two(k):
            scores, values = [], []
            for i in range(2):
                e = ent[r * TOPK + 2 * k + i]
                block = st[g].at[e]
                s = score(block[:, :HD], queries_of(r))
                if g == 1:
                    s = s + bias(PIECE, KEPT - HALF - PIECE + (2 * HALF - KEPT) * (1 - mine))
                scores.append(s)
                values.append(block[:, HD:])
            update(r, scores, values)

        loop(TOPK // 2, two)

    for half in range(2):
        block = q4.at[half, pl.ds(2 - base, 2)]
        arrived(block, q_s.at[half], q_r.at[half])
    m[...] = jnp.full_like(m, -1e30)
    l[...] = jnp.zeros_like(l)
    acc[...] = jnp.zeros_like(acc)
    for r in range(REQ_SECTION):
        s = score(kf[r], queries_of(r)) + bias(FROWS, FRESH * TOPK - TOPK * mine)
        update(r, [s], [vf[r]])
    s = score(ko[...], queries_of(mine))
    keys_at = lax.broadcasted_iota(jnp.int32, (QLEN, cols), 0)
    query_at = lax.rem(lax.broadcasted_iota(jnp.int32, (QLEN, cols), 1), QLEN)
    s = jnp.where(keys_at <= query_at, s, -jnp.inf)
    update(mine, [s], [vo[...]])

    def finish(r):
        done = (acc[r] / l[r]).astype(BF16)
        level = m[r] + jnp.log2(l[r])
        for j in range(4):
            span = slice(j * QLEN, (j + 1) * QLEN)
            oall[r, j // 2, pl.ds((j % 2) * HD, HD), :] = done[:, span]
            lall[r, j // 2, pl.ds(j % 2, 1), :] = level[:, span]
        push(sends, oall.at[r, 1 - mine], oin.at[r], ex_s.at[2 * r], ex_r.at[2 * r], pair)
        push(sends, lall.at[r, 1 - mine], lin.at[r], ex_s.at[2 * r + 1], ex_r.at[2 * r + 1], pair)

    def join(r):
        arrived(oin.at[r], ex_s.at[2 * r], ex_r.at[2 * r])
        arrived(lin.at[r], ex_s.at[2 * r + 1], ex_r.at[2 * r + 1])
        for j in range(2):
            a, b = lall[r, mine, pl.ds(j, 1), :], lin[r, pl.ds(j, 1), :]
            most = jnp.maximum(a, b)
            a, b = jnp.exp2(a - most), jnp.exp2(b - most)
            span = pl.ds(j * HD, HD)
            joined = oall[r, mine, span, :].astype(F32) * a + oin[r, span, :].astype(F32) * b
            joined = joined / (a + b)
            att[r * QLEN : (r + 1) * QLEN, j * HD : (j + 1) * HD] = joined.T.astype(BF16)

    size = REQ_SECTION * QLEN // BLOCKS
    part = size // 2
    width = xall.shape[3]

    def units(b, half, first, second, count):
        return xall.at[half, pl.ds(first * SIDE + second, count), pl.ds(b * part, part)]

    def compute(b):
        def one(k):
            xx = around(x_, 2 + k // SIDE)
            zz = around(z, 2 + lax.rem(k, SIDE))
            span = pl.ds(pl.multiple_of((zz * SIDE + xx) * width, width), width)
            got = jnp.dot(
                att[b * size : (b + 1) * size, :], wv[:, span], preferred_element_type=F32
            ).astype(BF16)
            xall[0, xx * SIDE + zz, pl.ds(b * part, part)] = got[:part]
            xall[1, zz * SIDE + xx, pl.ds(b * part, part)] = got[part:]

        loop(N_DEV, one)

    def out_push(s, src, dst, target):
        push(sends, src, dst, br_s.at[s], br_r.at[s], target)

    def first(b):
        for half in range(2):
            c, s = spot[half], 20 * b + 10 * half
            out_push(s, units(b, half, around(c, 2), 0, 2), bl1.at[b, half], ahead[half][0])
            out_push(s + 1, units(b, half, around(c, 2), 2, 2), br1.at[b, half], ahead[half][1])
            out_push(s + 2, units(b, half, around(c, 1), 2, 2), bl2.at[b, half, hi], ahead[half][0])
            out_push(s + 3, units(b, half, around(c, -1), 0, 2), br2.at[b, half, lo], ahead[half][1])

    def out_arrived(block, s):
        arrived(block, br_s.at[s], br_r.at[s])

    def second(b):
        for half in range(2):
            c, s = spot[half], 20 * b + 10 * half
            out_arrived(bl1.at[b, half], s)
            block = units(b, half, around(c, 1), 0, 2)
            block[...] = (block[...].astype(F32) + bl1[b, half].astype(F32)).astype(BF16)
            out_push(s + 4, block, bl2.at[b, half, lo], ahead[half][0])
            out_arrived(br1.at[b, half], s + 1)
            block = units(b, half, around(c, -1), 2, 2)
            block[...] = (block[...].astype(F32) + br1[b, half].astype(F32)).astype(BF16)
            out_push(s + 5, block, br2.at[b, half, hi], ahead[half][1])

    def third(b):
        for half in range(2):
            c, s = spot[half], 20 * b + 10 * half
            out_arrived(bl2.at[b, half, hi], s + 2)
            out_arrived(br2.at[b, half, lo], s + 3)
            out_arrived(bl2.at[b, half, lo], s + 4)
            out_arrived(br2.at[b, half, hi], s + 5)
            block = units(b, half, c, 0, SIDE)
            total = block[...].astype(F32) + bl2[b, half].astype(F32) + br2[b, half].astype(F32)
            block[...] = total.astype(BF16)
            for k in (1, 3, 2, 0):
                other = around(spot[1 - half], k)
                target = (after, other * SIDE + x_) if half == 0 else (after, z * SIDE + other)
                out_push(s + 6 + k, xall.at[half, c * SIDE + other, pl.ds(b * part, part)],
                         bz2.at[b, half, k], target)

    def fourth(b):
        for half in range(2):
            s = 20 * b + 10 * half
            total = None
            for k in range(SIDE):
                out_arrived(bz2.at[b, half, k], s + 6 + k)
                block = bz2[b, half, k].astype(F32)
                total = block if total is None else total + block
            outv[pl.ds(b * size + half * part, part), :] = total.astype(BF16)

    passages_wait(0)
    stored(0, 0)
    stored(1, 0)
    for copy in ag_sends:
        copy.wait_send()
    loads[9].wait()
    passages_wait(1)
    stored(0, 1)
    finish(0)
    stored(1, 1)
    finish(1)
    join(0)
    per = BLOCKS // REQ_SECTION
    for b in range(per):
        compute(b)
        first(b)
    join(1)
    for b in range(BLOCKS):
        if per + b < BLOCKS:
            compute(per + b)
            first(per + b)
        second(b)
        if b > 0:
            third(b - 1)
    third(BLOCKS - 1)
    for b in range(BLOCKS):
        fourth(b)
    done = pltpu.make_async_copy(outv, out, loc.at[10])
    done.start()
    for copy in sends:
        copy.wait_send()
    done.wait()


def layer(home, retrieved, order, x, hid, kvw, qw, ow, store, rec, freq, pos):
    anywhere = pl.BlockSpec(memory_space=pl.ANY)
    vmem = pl.BlockSpec(memory_space=pltpu.VMEM)
    smem = pl.BlockSpec(memory_space=pltpu.SMEM)
    dma = pltpu.SemaphoreType.DMA
    d_here = x.shape[1]
    cols = 4 * QLEN
    part = REQ_SECTION * QLEN // BLOCKS // 2
    width = ow.shape[1] // N_DEV
    assert width == d_here

    def bf16(*shape):
        return pltpu.VMEM(shape, BF16)

    def f32(*shape):
        return pltpu.VMEM(shape, F32)

    return pl.pallas_call(
        layer_kernel,
        out_shape=jax.ShapeDtypeStruct((REQ_SECTION * QLEN, width), BF16),
        in_specs=[smem] * 3 + [anywhere] * 6 + [vmem] * 3,
        out_specs=anywhere,
        scratch_shapes=[
            pltpu.SMEM((SLOTS,), jnp.int32),
            bf16(2, N_DEV, QLEN, d_here),
            bf16(*qw.shape),
            bf16(*kvw.shape),
            bf16(REQ_SECTION, GROUP, d_here),
            bf16(SIDE, SIDE, GROUP, HD),
            bf16(SIDE, SIDE, GROUP, HD),
            bf16(2, 2, GROUP, HD),
            bf16(2, 2, GROUP, HD),
            bf16(2, SIDE, GROUP, HD),
            bf16(2, SIDE, GROUP, HD),
            bf16(2, SIDE - 1, GROUP, HD),
            f32(2, QLEN, 2 * HD),
            bf16(*store.shape),
            bf16(2, N_DEV, CAP, PIECE, 2 * HD),
            bf16(N_DEV * CAP, PIECE, 2 * HD),
            bf16(N_DEV * CAP, PIECE, 2 * HD),
            bf16(REQ_SECTION, 4, QLEN, HD),
            bf16(REQ_SECTION, FROWS, HD),
            bf16(REQ_SECTION, FROWS, HD),
            bf16(QLEN, HD),
            bf16(QLEN, HD),
            f32(REQ_SECTION, HD, cols),
            f32(REQ_SECTION, 1, cols),
            f32(REQ_SECTION, 1, cols),
            bf16(REQ_SECTION, 2, 2 * HD, QLEN),
            f32(REQ_SECTION, 2, 8, QLEN),
            bf16(REQ_SECTION, 2 * HD, QLEN),
            f32(REQ_SECTION, 8, QLEN),
            bf16(*ow.shape),
            bf16(REQ_SECTION * QLEN, 2 * HD),
            bf16(BLOCKS, 2, 2, part, width),
            bf16(BLOCKS, 2, 2, part, width),
            bf16(BLOCKS, 2, SIDE, part, width),
            bf16(BLOCKS, 2, SIDE, part, width),
            bf16(BLOCKS, 2, SIDE, part, width),
            bf16(REQ_SECTION * QLEN, width),
            dma((11,)),
            dma((2,)),
            dma((40,)),
            dma((40,)),
            dma((18,)),
            dma((18,)),
            dma((2 * len(STEPS),)),
            dma((2 * len(STEPS),)),
            dma((2,)),
            dma((2,)),
            dma((4,)),
            dma((4,)),
            dma((20 * BLOCKS,)),
            dma((20 * BLOCKS,)),
        ],
        compiler_params=pltpu.CompilerParams(
            collective_id=0, has_side_effects=True, vmem_limit_bytes=63 * 2**20
        ),
        name="layer",
    )(home, retrieved, order, x, hid, kvw, qw, ow, store, rec, freq, pos)


def body(
    activations, q_weight, out_weight, kv_weight, passage_store,
    passage_home, retrieved, slot_order, recomputed, passage_hidden,
):
    mine = lax.rem(lax.axis_index("dev"), 2)
    half_dim = HD // 2
    frequency = ROPE_BASE ** (-(jnp.arange(half_dim, dtype=F32) * (2.0 / HD)))
    frequency = jnp.concatenate([frequency, frequency])[None]
    offsets = slot_order[0].reshape(SLOTS) * PASS_LEN
    fresh_pos = jnp.pad(recomputed[0].T + offsets, ((0, 2 * FRESH - RECOMP), (0, 0)))
    fresh_pos = jnp.where(mine == 0, fresh_pos[:FRESH], fresh_pos[FRESH:]).reshape(-1)
    token_pos = TOPK * PASS_LEN + jnp.arange(QLEN, dtype=jnp.int32)
    pos = jnp.concatenate([token_pos, fresh_pos]).astype(F32)[:, None]
    hidden = passage_hidden[0].transpose(1, 0, 2).reshape(RECOMP * SLOTS, -1)
    out = layer(
        passage_home, retrieved, slot_order, activations[0], hidden, kv_weight[0], q_weight[0],
        out_weight[0], passage_store[0], recomputed, frequency, pos,
    )
    return out[None]


def solution(mesh):
    in_specs = (
        P("section", None, "dev"),
        P("section", None, "dev"),
        P("section", "dev", None),
        P("section", "dev", None),
        P("section", "dev", None, None, None),
        P("section", None),
        P("section", None, None),
        P("section", None, None),
        P("section", None, None),
        P("section", None, None, "dev"),
    )
    out_specs = P("section", None, "dev")
    return jax.shard_map(body, mesh=mesh, in_specs=in_specs, out_specs=out_specs, check_vma=False)
```

```python
import functools

import jax
import jax.numpy as jnp
import numpy as np
from jax import lax
from jax.experimental import pallas as pl
from jax.experimental.pallas import tpu as pltpu
from jax.sharding import PartitionSpec as P

QH = 32
KVH = 8
HD = 128
PASS_LEN = 512
TOPK = 8
RECOMP = 77
REQ_SECTION = 2
QLEN = 256
SLOTS = 16
CAP = 2
PASS_DEV = 4
SIDE = 4
N_DEV = 16
FRESH = 39
GROUP = QLEN + FRESH * SLOTS
FROWS = 320
KEPT = PASS_LEN - RECOMP
HALF = 224
PIECES = (112, 64, 48)
STARTS = (0, 112, 176)
GROUPS = len(PIECES)
BLOCKS = 4
ROPE_BASE = 500000.0
MESH = pl.DeviceIdType.MESH
F32 = jnp.float32
BF16 = jnp.bfloat16
SCALE = HD**-0.5 * 1.4426950408889634


def lane_tables(angles):
    sign = jnp.where(lax.broadcasted_iota(jnp.int32, (1, HD), 1) < HD // 2, -1.0, 1.0)
    return jnp.cos(angles), jnp.sin(angles) * sign


def turned(v, cosine, sine):
    return v * cosine + pltpu.roll(v, HD // 2, axis=1) * sine


def place():
    d = lax.axis_index("dev")
    return lax.axis_index("section"), d // SIDE, lax.rem(d, SIDE)


def around(v, step):
    return lax.rem(v + step + SIDE, SIDE)


def remote(src, dst, send, recv, target):
    return pltpu.make_async_remote_copy(
        src_ref=src,
        dst_ref=dst,
        send_sem=send,
        recv_sem=recv,
        device_id=target,
        device_id_type=MESH,
    )


STEPS = (
    (0, 1), (0, 3), (1, 0), (3, 0), (1, 1), (3, 3), (1, 3), (3, 1),
    (0, 2), (2, 0), (2, 1), (2, 3), (1, 2), (3, 2), (2, 2),
)


def layer_kernel(
    home, retrieved, order, x, hid, kvw, qw, ow, store, rec, freq, out,
    ent, xall, qv, kvv, rows, pa, pb, l1, r1, l2, r2, z2, qacc,
    storev, out0, out1, out2, st0, st1, st2, q4, kf, vf, ko, vo, acc, m, l,
    angle, oall, lall, oin, lin, wv, att, bl1, br1, bl2, br2, bz2, outv,
    loc, own_s, ag_s, ag_r, rs_s, rs_r, st_s, st_r, q_s, q_r, ex_s, ex_r, br_s, br_r,
):
    sec = lax.axis_index("section")
    me = lax.axis_index("dev")
    z, x_ = me // SIDE, lax.rem(me, SIDE)
    sections = lax.axis_size("section")
    after, before = lax.rem(sec + 1, sections), lax.rem(sec + sections - 1, sections)
    mine = lax.rem(me, 2)

    def at(zz, xx):
        return (sec, zz * SIDE + xx)

    right, left = at(z, around(x_, 1)), at(z, around(x_, -1))
    down, up = at(around(z, 1), x_), at(around(z, -1), x_)
    pair = (sec, me + 1 - 2 * mine)
    ahead = [(right, left), (down, up)]
    spot = [x_, z]

    greeted = [(sec, lax.rem(me + k, N_DEV)) for k in range(1, N_DEV)]
    for s in (after, before):
        greeted.append((s, me))
        for k in range(1, SIDE):
            greeted.append((s, z * SIDE + around(x_, k)))
            greeted.append((s, around(z, k) * SIDE + x_))
    barrier = pltpu.get_barrier_semaphore()
    for target in greeted:
        pl.semaphore_signal(barrier, inc=1, device_id=target, device_id_type=MESH)

    first_rows, last_rows = FRESH * SLOTS, (RECOMP - FRESH) * SLOTS
    loads = [
        pltpu.make_async_copy(kvw, kvv, loc.at[0]),
        pltpu.make_async_copy(x.at[pl.ds(0, QLEN)], rows.at[0, pl.ds(0, QLEN)], loc.at[1]),
        pltpu.make_async_copy(x.at[pl.ds(QLEN, QLEN)], rows.at[1, pl.ds(0, QLEN)], loc.at[2]),
        pltpu.make_async_copy(
            hid.at[pl.ds(0, first_rows)], rows.at[0, pl.ds(QLEN, first_rows)], loc.at[3]
        ),
        pltpu.make_async_copy(
            hid.at[pl.ds(first_rows, last_rows)], rows.at[1, pl.ds(QLEN, last_rows)], loc.at[4]
        ),
        pltpu.make_async_copy(store, storev, loc.at[5]),
        pltpu.make_async_copy(qw, qv, loc.at[6]),
        pltpu.make_async_copy(x.at[pl.ds(0, QLEN)], xall.at[0, me], loc.at[7]),
        pltpu.make_async_copy(x.at[pl.ds(QLEN, QLEN)], xall.at[1, me], loc.at[8]),
        pltpu.make_async_copy(ow, wv, loc.at[9]),
    ]
    for load in loads:
        load.start()
    rest = rows.at[1, pl.ds(QLEN + last_rows, GROUP - QLEN - last_rows)]
    rest[...] = jnp.zeros_like(rest)
    pl.semaphore_wait(barrier, len(greeted))

    def chunk(half, first, second):
        if half == 0:
            return around(z, second) * SIDE + around(x_, first)
        return around(z, first) * SIDE + around(x_, second)

    top, bottom = pl.ds(0, QLEN // 2), pl.ds(QLEN // 2, QLEN // 2)
    whole = pl.ds(0, QLEN)
    sends = []

    def ag(half, src, span, sem, target, own=False):
        to = xall.at[half, src, span]
        frm = x.at[pl.ds(half * QLEN, QLEN)] if own else to
        remote(frm, to, ag_s.at[half], ag_r.at[15 * half + sem], target).start()

    def ag_wait(half, src, sem):
        to = xall.at[half, src, whole]
        remote(to, to, ag_s.at[half], ag_r.at[15 * half + sem], right).wait_recv()

    for half in range(2):
        ag(half, me, whole, 0, ahead[half][0], True)
        ag(half, me, whole, 1, ahead[half][1], True)
    for half in range(2):
        ag(half, me, whole, 3, ahead[1 - half][0], True)
        ag(half, me, whole, 4, ahead[1 - half][1], True)

    def push(group, src, dst, send, recv, target):
        copy = remote(src, dst, send, recv, target)
        copy.start()
        group.append(copy)

    def arrived(block, send, recv):
        remote(block, block, send, recv, right).wait_recv()

    def project(xx, zz):
        head = 2 * zz + xx // 2
        span = pl.ds(pl.multiple_of(head * 2 * HD, 2 * HD), 2 * HD)
        part = jnp.dot(rows[lax.rem(xx, 2)], kvv[:, span], preferred_element_type=F32)
        part = part.astype(BF16)
        pa[xx, zz] = part[:, :HD]
        pb[zz, xx] = part[:, HD:]

    def loop(count, step):
        def one(k, carry):
            step(k)
            return carry

        lax.fori_loop(0, count, one, 0)

    def skip_two(t):
        return t + t // 2

    parts = [pa, pb]
    lo, hi = pl.ds(0, 2), pl.ds(2, 2)

    def rs(half, src, dst, sem, target):
        remote(src, dst, rs_s.at[2 * half + sem // 4], rs_r.at[5 * half + sem], target).start()

    def rs_arrived(half, block, sem):
        arrived(block, rs_s.at[2 * half + sem // 4], rs_r.at[5 * half + sem])

    def rs_first(half):
        p, c = parts[half], spot[half]
        rs(half, p.at[around(c, 2), lo], l1.at[half], 0, ahead[half][0])
        rs(half, p.at[around(c, 2), hi], r1.at[half], 1, ahead[half][1])

    for k in range(5):
        loads[k].wait()
    loop(SIDE, lambda k: project(around(x_, 2), around(z, k)))
    rs_first(0)
    loop(SIDE - 1, lambda k: project(around(x_, skip_two(k)), around(z, 2)))
    rs_first(1)
    loop(9, lambda k: project(around(x_, skip_two(k // 3)), around(z, skip_two(lax.rem(k, 3)))))

    for half in range(2):
        src = chunk(half, -1, 0)
        ag_wait(half, src, 0)
        ag(half, src, top, 2, ahead[half][0])
        ag(half, src, whole, 6, ahead[1 - half][0])
        ag(half, src, whole, 7, ahead[1 - half][1])
        src = chunk(half, 1, 0)
        ag_wait(half, src, 1)
        ag(half, src, bottom, 2, ahead[half][1])
        ag(half, src, whole, 9, ahead[1 - half][0])
        ag(half, src, whole, 10, ahead[1 - half][1])
    for half in range(2):
        p, c = parts[half], spot[half]
        rs(half, p.at[around(c, 1), hi], l2.at[half, hi], 2, ahead[half][0])
        rs(half, p.at[around(c, -1), lo], r2.at[half, lo], 3, ahead[half][1])

    homes = [home[0, retrieved[0, j // TOPK, j % TOPK]] for j in range(SLOTS)]
    owners = [h // PASS_DEV for h in homes]
    entries = []
    for j in range(SLOTS):
        rank = jnp.int32(0)
        for i in range(j):
            rank = rank + jnp.where(owners[i] == owners[j], 1, 0)
        entries.append(owners[j] * CAP + rank)
        ent[j] = entries[j]
    frequency = freq[...]
    sent, st = [out0, out1, out2], [st0, st1, st2]
    loads[5].wait()
    for c in range(CAP):
        row, slot, offset = jnp.int32(0), jnp.int32(0), jnp.int32(0)
        for j in range(SLOTS):
            hit = entries[j] == me * CAP + c
            row = jnp.where(hit, lax.rem(homes[j], PASS_DEV), row)
            slot = jnp.where(hit, j, slot)
            offset = jnp.where(hit, order[0, j // TOPK, j % TOPK] * PASS_LEN, offset)
        dropped = rec[0, pl.ds(slot, 1), :]
        ahead_of = (dropped - lax.broadcasted_iota(jnp.int32, (1, RECOMP), 1)).astype(F32)
        index = lax.broadcasted_iota(jnp.int32, (2 * HALF, RECOMP), 0).astype(F32)
        count = jnp.sum(jnp.where(ahead_of <= index, 1.0, 0.0), axis=1, keepdims=True)
        keep = index[:, :1] + count
        lanes = lax.broadcasted_iota(jnp.int32, (2 * HALF, PASS_LEN), 1).astype(F32)
        pick = jnp.where(lanes == keep, 1.0, 0.0).astype(BF16)
        cosine, sine = lane_tables(frequency * offset.astype(F32))

        def one_head(h):
            kept = jnp.dot(pick, storev[row, h], preferred_element_type=F32)
            keys = turned(kept[:, :HD], cosine, sine).astype(BF16)
            values = kept[:, HD:].astype(BF16)
            for half in range(2):
                for g in range(GROUPS):
                    start = half * HALF + STARTS[g]
                    to = sent[g].at[2 * h + half, c]
                    to[:, :HD] = keys[start : start + PIECES[g]]
                    to[:, HD:] = values[start : start + PIECES[g]]

        loop(KVH, one_head)

    for g in range(GROUPS):
        copy = pltpu.make_async_copy(
            sent[g].at[me], st[g].at[pl.ds(2 * me, CAP)], own_s.at[g]
        )
        copy.start()

    def passages(g):
        for dz, dx in STEPS:
            other = around(z, dz) * SIDE + around(x_, dx)
            to = st[g].at[pl.ds(2 * me, CAP)]
            remote(sent[g].at[other], to, st_s.at[g], st_r.at[g], (sec, other)).start()

    def passages_wait(g):
        pltpu.make_async_copy(
            sent[g].at[me], st[g].at[pl.ds(2 * me, CAP)], own_s.at[g]
        ).wait()
        arrived(st[g].at[pl.ds(0, CAP * (N_DEV - 1))], st_s.at[g], st_r.at[g])

    for half in range(2):
        src = chunk(half, 2, 0)
        ag_wait(half, src, 2)
        ag(half, src, whole, 12, ahead[1 - half][0])
        ag(half, src, whole, 13, ahead[1 - half][1])

    def second_axis(k, first):
        b = 3 + 3 * k
        for half in range(2):
            src = chunk(half, first, -1)
            ag_wait(half, src, b)
            ag(half, src, top, b + 2, ahead[1 - half][0])
            src = chunk(half, first, 1)
            ag_wait(half, src, b + 1)
            ag(half, src, bottom, b + 2, ahead[1 - half][1])

    second_axis(0, 0)

    for half in range(2):
        p, c = parts[half], spot[half]
        rs_arrived(half, l1.at[half], 0)
        block = p.at[around(c, 1), lo]
        block[...] = (block[...].astype(F32) + l1[half].astype(F32)).astype(BF16)
        rs(half, block, l2.at[half, lo], 2, ahead[half][0])
        rs_arrived(half, r1.at[half], 1)
        block = p.at[around(c, -1), hi]
        block[...] = (block[...].astype(F32) + r1[half].astype(F32)).astype(BF16)
        rs(half, block, r2.at[half, hi], 3, ahead[half][1])

    second_axis(1, -1)
    second_axis(2, 1)
    second_axis(3, 2)

    for half in range(2):
        p, c = parts[half], spot[half]
        rs_arrived(half, l2.at[half], 2)
        rs_arrived(half, r2.at[half], 3)
        for u in range(SIDE):
            block = p.at[c, u]
            total = block[...].astype(F32) + l2[half, u].astype(F32) + r2[half, u].astype(F32)
            block[...] = total.astype(BF16)
        for k in (1, 3, 2):
            other = around(spot[1 - half], k)
            target = at(other, x_) if half == 0 else at(z, other)
            rs(half, p.at[c, other], z2.at[half, k - 1], 4, target)
    passages(0)

    for k in (6, 7, 8):
        loads[k].wait()
    for half in range(2):
        for k in range(SIDE):
            ag_wait(half, chunk(half, (0, -1, 1, 2)[k], 2), 5 + 3 * k)

    def project_queries(k):
        span = pl.ds(pl.multiple_of(k * 2 * QLEN, 2 * QLEN), 2 * QLEN)
        weight = qv[span, :]
        for half in range(2):
            qacc[half] += jnp.dot(xall[half, k], weight, preferred_element_type=F32)

    qacc[...] = jnp.zeros_like(qacc)
    loop(N_DEV, project_queries)
    token_at = lax.broadcasted_iota(jnp.int32, (QLEN, 1), 0) + TOPK * PASS_LEN
    token_angles = token_at.astype(F32) * frequency
    cosine, sine = lane_tables(token_angles)
    base = 2 * mine
    for half in range(2):
        for j in range(2):
            head = turned(qacc[half, :, j * HD : (j + 1) * HD], cosine, sine)
            q4[half, base + j] = head.astype(BF16)
        block = q4.at[half, pl.ds(base, 2)]
        push(sends, block, block, q_s.at[half], q_r.at[half], pair)

    for g in range(1, GROUPS):
        passages(g)

    slot_at = lax.broadcasted_iota(jnp.int32, (SLOTS, 1), 0)
    offsets = jnp.zeros((SLOTS, 1), jnp.int32)
    for j in range(SLOTS):
        offsets = jnp.where(slot_at == j, order[0, j // TOPK, j % TOPK] * PASS_LEN, offsets)
    places = rec[0] + offsets
    angle[pl.ds(0, QLEN)] = token_angles
    for i in range(FRESH):
        here = places[:, i : i + 1]
        if FRESH + i < RECOMP:
            here = jnp.where(mine == 0, here, places[:, FRESH + i : FRESH + i + 1])
        angle[pl.ds(QLEN + i * SLOTS, SLOTS)] = here.astype(F32) * frequency
    cosine, sine = lane_tables(angle[...])
    for half in range(2):
        p, c = parts[half], spot[half]
        total = p[c, spot[1 - half]].astype(F32)
        rs_arrived(half, z2.at[half], 4)
        for k in range(1, SIDE):
            total += z2[half, k - 1].astype(F32)
        total = total.astype(BF16).astype(F32)
        if half == 0:
            total = turned(total, cosine, sine)
        own_to, fresh_to = (ko, kf) if half == 0 else (vo, vf)
        own_to[...] = total[:QLEN].astype(BF16)
        fresh = total[QLEN:].reshape(FRESH, SLOTS, HD)
        for r in range(REQ_SECTION):
            rows_of = fresh[:, r * TOPK : (r + 1) * TOPK].reshape(FRESH * TOPK, HD)
            filler = jnp.zeros((FROWS - FRESH * TOPK, HD), F32)
            fresh_to[r] = jnp.concatenate([rows_of, filler], axis=0).astype(BF16)

    cols = 4 * QLEN

    def score(keys, queries):
        s = lax.dot_general(
            keys, queries, (((1,), (1,)), ((), ())), preferred_element_type=F32
        )
        return s * SCALE

    def update(r, scores, values):
        old = m[r]
        new = old
        for s in scores:
            new = jnp.maximum(new, jnp.max(s, axis=0, keepdims=True))
        scale = jnp.exp2(old - new)
        total, mixed = l[r] * scale, acc[r] * scale
        for s, v in zip(scores, values):
            weights = jnp.exp2(s - new)
            total = total + jnp.sum(weights, axis=0, keepdims=True)
            mixed = mixed + lax.dot_general(
                v, weights.astype(BF16), (((0,), (0,)), ((), ())), preferred_element_type=F32
            )
        m[r], l[r], acc[r] = new, total, mixed

    def bias(count, valid):
        index = lax.broadcasted_iota(jnp.int32, (count, 1), 0)
        return jnp.where(index < valid, 0.0, -jnp.inf)

    def queries_of(r):
        return q4[r].reshape(cols, HD)

    def stored(r, g):
        many = 2 if g == 0 else 4

        def some(k):
            scores, values = [], []
            for i in range(many):
                e = ent[r * TOPK + many * k + i]
                block = st[g].at[e]
                s = score(block[:, :HD], queries_of(r))
                if g == GROUPS - 1:
                    s = s + bias(PIECES[g], PIECES[g] - (2 * HALF - KEPT) * mine)
                scores.append(s)
                values.append(block[:, HD:])
            update(r, scores, values)

        loop(TOPK // many, some)

    for half in range(2):
        block = q4.at[half, pl.ds(2 - base, 2)]
        arrived(block, q_s.at[half], q_r.at[half])
    m[...] = jnp.full_like(m, -1e30)
    l[...] = jnp.zeros_like(l)
    acc[...] = jnp.zeros_like(acc)
    for r in range(REQ_SECTION):
        s = score(kf[r], queries_of(r)) + bias(FROWS, FRESH * TOPK - TOPK * mine)
        update(r, [s], [vf[r]])
    s = score(ko[...], queries_of(mine))
    keys_at = lax.broadcasted_iota(jnp.int32, (QLEN, cols), 0)
    query_at = lax.rem(lax.broadcasted_iota(jnp.int32, (QLEN, cols), 1), QLEN)
    s = jnp.where(keys_at <= query_at, s, -jnp.inf)
    update(mine, [s], [vo[...]])

    def finish(r):
        done = (acc[r] / l[r]).astype(BF16)
        level = m[r] + jnp.log2(l[r])
        for j in range(4):
            span = slice(j * QLEN, (j + 1) * QLEN)
            oall[r, j // 2, pl.ds((j % 2) * HD, HD), :] = done[:, span]
            lall[r, j // 2, pl.ds(j % 2, 1), :] = level[:, span]
        push(sends, oall.at[r, 1 - mine], oin.at[r], ex_s.at[2 * r], ex_r.at[2 * r], pair)
        push(sends, lall.at[r, 1 - mine], lin.at[r], ex_s.at[2 * r + 1], ex_r.at[2 * r + 1], pair)

    def join(r):
        arrived(oin.at[r], ex_s.at[2 * r], ex_r.at[2 * r])
        arrived(lin.at[r], ex_s.at[2 * r + 1], ex_r.at[2 * r + 1])
        for j in range(2):
            a, b = lall[r, mine, pl.ds(j, 1), :], lin[r, pl.ds(j, 1), :]
            most = jnp.maximum(a, b)
            a, b = jnp.exp2(a - most), jnp.exp2(b - most)
            span = pl.ds(j * HD, HD)
            joined = oall[r, mine, span, :].astype(F32) * a + oin[r, span, :].astype(F32) * b
            joined = joined / (a + b)
            att[r * QLEN : (r + 1) * QLEN, j * HD : (j + 1) * HD] = joined.T.astype(BF16)

    size = REQ_SECTION * QLEN // BLOCKS
    part = size // 2
    width = xall.shape[3]

    def units(b, half, first, second, count):
        return xall.at[half, pl.ds(first * SIDE + second, count), pl.ds(b * part, part)]

    def compute(b, xx, zz):
        span = pl.ds(pl.multiple_of((zz * SIDE + xx) * width, width), width)
        got = jnp.dot(
            att[b * size : (b + 1) * size, :], wv[:, span], preferred_element_type=F32
        ).astype(BF16)
        xall[0, xx * SIDE + zz, pl.ds(b * part, part)] = got[:part]
        xall[1, zz * SIDE + xx, pl.ds(b * part, part)] = got[part:]

    def out_push(b, half, sem, src, dst, target):
        s = 2 * b + half
        remote(src, dst, br_s.at[s], br_r.at[5 * s + sem], target).start()

    def out_arrived(b, half, sem, block):
        s = 2 * b + half
        arrived(block, br_s.at[s], br_r.at[5 * s + sem])

    def first(b):
        loop(SIDE, lambda k: compute(b, around(x_, 2), around(z, k)))
        loop(SIDE - 1, lambda k: compute(b, around(x_, skip_two(k)), around(z, 2)))
        for half in range(2):
            c = spot[half]
            out_push(b, half, 0, units(b, half, around(c, 2), 0, 2), bl1.at[b, half], ahead[half][0])
            out_push(b, half, 1, units(b, half, around(c, 2), 2, 2), br1.at[b, half], ahead[half][1])
        loop(
            9,
            lambda k: compute(
                b, around(x_, skip_two(k // 3)), around(z, skip_two(lax.rem(k, 3)))
            ),
        )
        for half in range(2):
            c = spot[half]
            out_push(b, half, 2, units(b, half, around(c, 1), 2, 2), bl2.at[b, half, hi], ahead[half][0])
            out_push(b, half, 3, units(b, half, around(c, -1), 0, 2), br2.at[b, half, lo], ahead[half][1])

    def second(b):
        for half in range(2):
            c = spot[half]
            out_arrived(b, half, 0, bl1.at[b, half])
            block = units(b, half, around(c, 1), 0, 2)
            block[...] = (block[...].astype(F32) + bl1[b, half].astype(F32)).astype(BF16)
            out_push(b, half, 2, block, bl2.at[b, half, lo], ahead[half][0])
            out_arrived(b, half, 1, br1.at[b, half])
            block = units(b, half, around(c, -1), 2, 2)
            block[...] = (block[...].astype(F32) + br1[b, half].astype(F32)).astype(BF16)
            out_push(b, half, 3, block, br2.at[b, half, hi], ahead[half][1])

    def third(b):
        for half in range(2):
            c = spot[half]
            out_arrived(b, half, 2, bl2.at[b, half])
            out_arrived(b, half, 3, br2.at[b, half])
            block = units(b, half, c, 0, SIDE)
            total = block[...].astype(F32) + bl2[b, half].astype(F32) + br2[b, half].astype(F32)
            block[...] = total.astype(BF16)
            for k in (1, 3, 2, 0):
                other = around(spot[1 - half], k)
                target = (after, other * SIDE + x_) if half == 0 else (after, z * SIDE + other)
                src = xall.at[half, c * SIDE + other, pl.ds(b * part, part)]
                out_push(b, half, 4, src, bz2.at[b, half, k], target)

    results = []

    def fourth(b):
        if b > 1:
            results[b - 2].wait()
        for half in range(2):
            out_arrived(b, half, 4, bz2.at[b, half])
            total = bz2[b, half, 0].astype(F32)
            for k in range(1, SIDE):
                total += bz2[b, half, k].astype(F32)
            outv[b % 2, pl.ds(half * part, part), :] = total
        to = out.at[pl.ds(b * size, size)]
        results.append(pltpu.make_async_copy(outv.at[b % 2], to, loc.at[10 + b]))
        results[b].start()

    for g in range(GROUPS - 1):
        passages_wait(g)
        stored(0, g)
        stored(1, g)
    for half in range(2):
        gone = xall.at[half, pl.ds(0, N_DEV - 1)]
        remote(gone, gone, ag_s.at[half], ag_r.at[0], right).wait_send()
    loads[9].wait()
    passages_wait(GROUPS - 1)
    stored(0, GROUPS - 1)
    finish(0)
    stored(1, GROUPS - 1)
    finish(1)
    join(0)
    per = BLOCKS // REQ_SECTION
    for b in range(per):
        first(b)
    join(1)
    for b in range(BLOCKS):
        if per + b < BLOCKS:
            first(per + b)
        second(b)
        if b > 0:
            third(b - 1)
    third(BLOCKS - 1)
    for b in range(BLOCKS):
        fourth(b)
    for copy in sends:
        copy.wait_send()

    def gone(block, sem):
        remote(block, block, sem, br_r.at[0], right).wait_send()

    for half in range(2):
        gone(parts[half].at[pl.ds(0, SIDE - 1)], rs_s.at[2 * half])
        gone(parts[half].at[0, pl.ds(0, SIDE - 1)], rs_s.at[2 * half + 1])
        for b in range(BLOCKS):
            gone(units(b, half, 0, 0, N_DEV), br_s.at[2 * b + half])
    for g in range(GROUPS):
        gone(sent[g].at[pl.ds(0, N_DEV - 1)], st_s.at[g])
    for copy in results[-2:]:
        copy.wait()


def layer(home, retrieved, order, x, hid, kvw, qw, ow, store, rec, freq):
    anywhere = pl.BlockSpec(memory_space=pl.ANY)
    vmem = pl.BlockSpec(memory_space=pltpu.VMEM)
    smem = pl.BlockSpec(memory_space=pltpu.SMEM)
    dma = pltpu.SemaphoreType.DMA
    d_here = x.shape[1]
    cols = 4 * QLEN
    part = REQ_SECTION * QLEN // BLOCKS // 2
    width = ow.shape[1] // N_DEV
    assert width == d_here

    def bf16(*shape):
        return pltpu.VMEM(shape, BF16)

    def f32(*shape):
        return pltpu.VMEM(shape, F32)

    return pl.pallas_call(
        layer_kernel,
        out_shape=jax.ShapeDtypeStruct((REQ_SECTION * QLEN, width), F32),
        in_specs=[smem] * 3 + [anywhere] * 6 + [vmem] * 2,
        out_specs=anywhere,
        scratch_shapes=[
            pltpu.SMEM((SLOTS,), jnp.int32),
            bf16(2, N_DEV, QLEN, d_here),
            bf16(*qw.shape),
            bf16(*kvw.shape),
            bf16(REQ_SECTION, GROUP, d_here),
            bf16(SIDE, SIDE, GROUP, HD),
            bf16(SIDE, SIDE, GROUP, HD),
            bf16(2, 2, GROUP, HD),
            bf16(2, 2, GROUP, HD),
            bf16(2, SIDE, GROUP, HD),
            bf16(2, SIDE, GROUP, HD),
            bf16(2, SIDE - 1, GROUP, HD),
            f32(2, QLEN, 2 * HD),
            bf16(*store.shape),
            *[bf16(N_DEV, CAP, piece, 2 * HD) for piece in PIECES],
            *[bf16(N_DEV * CAP, piece, 2 * HD) for piece in PIECES],
            bf16(REQ_SECTION, 4, QLEN, HD),
            bf16(REQ_SECTION, FROWS, HD),
            bf16(REQ_SECTION, FROWS, HD),
            bf16(QLEN, HD),
            bf16(QLEN, HD),
            f32(REQ_SECTION, HD, cols),
            f32(REQ_SECTION, 1, cols),
            f32(REQ_SECTION, 1, cols),
            f32(GROUP, HD),
            bf16(REQ_SECTION, 2, 2 * HD, QLEN),
            f32(REQ_SECTION, 2, 8, QLEN),
            bf16(REQ_SECTION, 2 * HD, QLEN),
            f32(REQ_SECTION, 8, QLEN),
            bf16(*ow.shape),
            bf16(REQ_SECTION * QLEN, 2 * HD),
            bf16(BLOCKS, 2, 2, part, width),
            bf16(BLOCKS, 2, 2, part, width),
            bf16(BLOCKS, 2, SIDE, part, width),
            bf16(BLOCKS, 2, SIDE, part, width),
            bf16(BLOCKS, 2, SIDE, part, width),
            f32(2, 2 * part, width),
            dma((10 + BLOCKS,)),
            dma((GROUPS,)),
            dma((2,)),
            dma((30,)),
            dma((4,)),
            dma((10,)),
            dma((GROUPS,)),
            dma((GROUPS,)),
            dma((2,)),
            dma((2,)),
            dma((4,)),
            dma((4,)),
            dma((2 * BLOCKS,)),
            dma((10 * BLOCKS,)),
        ],
        compiler_params=pltpu.CompilerParams(
            collective_id=0, has_side_effects=True, vmem_limit_bytes=63 * 2**20
        ),
        name="layer",
    )(home, retrieved, order, x, hid, kvw, qw, ow, store, rec, freq)


def body(
    activations, q_weight, out_weight, kv_weight, passage_store,
    passage_home, retrieved, slot_order, recomputed, passage_hidden,
):
    exponents = -np.arange(HD // 2, dtype=np.float32) * np.float32(2.0 / HD)
    frequency = np.float32(ROPE_BASE) ** exponents
    frequency = jnp.asarray(np.concatenate([frequency, frequency])[None])
    hidden = passage_hidden[0].transpose(1, 0, 2).reshape(RECOMP * SLOTS, -1)
    out = layer(
        passage_home, retrieved, slot_order, activations[0], hidden, kv_weight[0], q_weight[0],
        out_weight[0], passage_store[0], recomputed, frequency,
    )
    return out.astype(BF16)[None]


def solution(mesh):
    in_specs = (
        P("section", None, "dev"),
        P("section", None, "dev"),
        P("section", "dev", None),
        P("section", "dev", None),
        P("section", "dev", None, None, None),
        P("section", None),
        P("section", None, None),
        P("section", None, None),
        P("section", None, None),
        P("section", None, None, "dev"),
    )
    out_specs = P("section", None, "dev")
    return jax.shard_map(body, mesh=mesh, in_specs=in_specs, out_specs=out_specs, check_vma=False)
```

```python
import functools

import jax
import jax.numpy as jnp
import numpy as np
from jax import lax
from jax.experimental import pallas as pl
from jax.experimental.pallas import tpu as pltpu
from jax.sharding import PartitionSpec as P

QH = 32
KVH = 8
HD = 128
PASS_LEN = 512
TOPK = 8
RECOMP = 77
REQ_SECTION = 2
QLEN = 256
SLOTS = 16
CAP = 2
PASS_DEV = 4
SIDE = 4
N_DEV = 16
FRESH = 39
GROUP = QLEN + FRESH * SLOTS
FROWS = 320
KEPT = PASS_LEN - RECOMP
HALF = 224
PIECES = (128, 64, 32)
STARTS = (0, 128, 192)
GROUPS = len(PIECES)
BLOCKS = 4
FIRSTS = ((0,), (1,))
ROPE_BASE = 500000.0
MESH = pl.DeviceIdType.MESH
F32 = jnp.float32
BF16 = jnp.bfloat16
SCALE = HD**-0.5 * 1.4426950408889634


def lane_tables(angles):
    sign = jnp.where(lax.broadcasted_iota(jnp.int32, (1, HD), 1) < HD // 2, -1.0, 1.0)
    return jnp.cos(angles), jnp.sin(angles) * sign


def turned(v, cosine, sine):
    return v * cosine + pltpu.roll(v, HD // 2, axis=1) * sine


def place():
    d = lax.axis_index("dev")
    return lax.axis_index("section"), d // SIDE, lax.rem(d, SIDE)


def around(v, step):
    return lax.rem(v + step + SIDE, SIDE)


def remote(src, dst, send, recv, target):
    return pltpu.make_async_remote_copy(
        src_ref=src,
        dst_ref=dst,
        send_sem=send,
        recv_sem=recv,
        device_id=target,
        device_id_type=MESH,
    )


STEPS = (
    (1, 1), (3, 3), (0, 2), (1, 3), (3, 1), (2, 0), (2, 1), (0, 3),
    (3, 2), (1, 0), (2, 3), (0, 1), (1, 2), (3, 0), (2, 2),
)


def layer_kernel(
    home, retrieved, order, x, hid, kvw, qw, ow, store, rec, freq, out,
    ent, xall, qv, kvv, rows, pa, pb, l1, r1, l2, r2, z1, z2, qacc,
    storev, out0, out1, out2, st0, st1, st2, q4, kf, vf, ko, vo, acc, m, l,
    angle, oall, lall, oin, lin, wv, att, bl1, br1, bl2, br2, bz2, outv,
    loc, own_s, ag_s, ag_r, rs_s, rs_r, st_s, st_r, q_s, q_r, ex_s, ex_r, br_s, br_r,
):
    sec = lax.axis_index("section")
    me = lax.axis_index("dev")
    z, x_ = me // SIDE, lax.rem(me, SIDE)
    sections = lax.axis_size("section")
    after, before = lax.rem(sec + 1, sections), lax.rem(sec + sections - 1, sections)
    mine = lax.rem(me, 2)

    def at(zz, xx):
        return (sec, zz * SIDE + xx)

    right, left = at(z, around(x_, 1)), at(z, around(x_, -1))
    down, up = at(around(z, 1), x_), at(around(z, -1), x_)
    pair = (sec, me + 1 - 2 * mine)
    ahead = [(right, left), (down, up)]
    spot = [x_, z]

    greeted = [(sec, lax.rem(me + k, N_DEV)) for k in range(1, N_DEV)]
    for s in (after, before):
        greeted.append((s, me))
        for k in range(1, SIDE):
            greeted.append((s, z * SIDE + around(x_, k)))
            greeted.append((s, around(z, k) * SIDE + x_))
    barrier = pltpu.get_barrier_semaphore()
    for target in greeted:
        pl.semaphore_signal(barrier, inc=1, device_id=target, device_id_type=MESH)

    first_rows, last_rows = FRESH * SLOTS, (RECOMP - FRESH) * SLOTS
    loads = [
        pltpu.make_async_copy(kvw, kvv, loc.at[0]),
        pltpu.make_async_copy(x.at[pl.ds(0, QLEN)], rows.at[0, pl.ds(0, QLEN)], loc.at[1]),
        pltpu.make_async_copy(x.at[pl.ds(QLEN, QLEN)], rows.at[1, pl.ds(0, QLEN)], loc.at[2]),
        pltpu.make_async_copy(
            hid.at[pl.ds(0, first_rows)], rows.at[0, pl.ds(QLEN, first_rows)], loc.at[3]
        ),
        pltpu.make_async_copy(
            hid.at[pl.ds(first_rows, last_rows)], rows.at[1, pl.ds(QLEN, last_rows)], loc.at[4]
        ),
        pltpu.make_async_copy(store, storev, loc.at[5]),
        pltpu.make_async_copy(qw, qv, loc.at[6]),
        pltpu.make_async_copy(x.at[pl.ds(0, QLEN)], xall.at[0, me], loc.at[7]),
        pltpu.make_async_copy(x.at[pl.ds(QLEN, QLEN)], xall.at[1, me], loc.at[8]),
        pltpu.make_async_copy(ow, wv, loc.at[9]),
    ]
    for load in loads:
        load.start()
    rest = rows.at[1, pl.ds(QLEN + last_rows, GROUP - QLEN - last_rows)]
    rest[...] = jnp.zeros_like(rest)
    pl.semaphore_wait(barrier, len(greeted))

    def chunk(half, first, second):
        if half == 0:
            return around(z, second) * SIDE + around(x_, first)
        return around(z, first) * SIDE + around(x_, second)

    top, bottom = pl.ds(0, QLEN // 2), pl.ds(QLEN // 2, QLEN // 2)
    whole = pl.ds(0, QLEN)
    sends = []

    def ag(half, src, span, sem, target, own=False):
        to = xall.at[half, src, span]
        frm = x.at[pl.ds(half * QLEN, QLEN)] if own else to
        remote(frm, to, ag_s.at[half], ag_r.at[15 * half + sem], target).start()

    def ag_wait(half, src, sem):
        to = xall.at[half, src, whole]
        remote(to, to, ag_s.at[half], ag_r.at[15 * half + sem], right).wait_recv()

    for half in range(2):
        ag(half, me, whole, 0, ahead[half][0], True)
        ag(half, me, whole, 1, ahead[half][1], True)
    for half in range(2):
        ag(half, me, whole, 3, ahead[1 - half][0], True)
        ag(half, me, whole, 4, ahead[1 - half][1], True)

    def push(group, src, dst, send, recv, target):
        copy = remote(src, dst, send, recv, target)
        copy.start()
        group.append(copy)

    def arrived(block, send, recv):
        remote(block, block, send, recv, right).wait_recv()

    def project(xx, zz):
        head = 2 * zz + xx // 2
        span = pl.ds(pl.multiple_of(head * 2 * HD, 2 * HD), 2 * HD)
        part = jnp.dot(rows[lax.rem(xx, 2)], kvv[:, span], preferred_element_type=F32)
        part = part.astype(BF16)
        pa[xx, zz] = part[:, :HD]
        pb[zz, xx] = part[:, HD:]

    def loop(count, step):
        def one(k, carry):
            step(k)
            return carry

        lax.fori_loop(0, count, one, 0)

    def skip_two(t):
        return t + t // 2

    parts = [pa, pb]
    lo, hi = pl.ds(0, 2), pl.ds(2, 2)

    def rs(half, src, dst, sem, target):
        remote(src, dst, rs_s.at[2 * half + sem // 4], rs_r.at[8 * half + sem], target).start()

    def rs_arrived(half, block, sem):
        arrived(block, rs_s.at[2 * half + sem // 4], rs_r.at[8 * half + sem])

    upper, lower = pl.ds(0, GROUP // 32 * 16), pl.ds(GROUP // 32 * 16, GROUP - GROUP // 32 * 16)

    def rs_first(half):
        p, c = parts[half], spot[half]
        rs(half, p.at[around(c, 2), lo], l1.at[half], 0, ahead[half][0])
        rs(half, p.at[around(c, 2), hi], r1.at[half], 1, ahead[half][1])

    for k in range(5):
        loads[k].wait()
    loop(SIDE, lambda k: project(around(x_, 2), around(z, k)))
    rs_first(0)
    loop(SIDE - 1, lambda k: project(around(x_, skip_two(k)), around(z, 2)))
    rs_first(1)
    loop(9, lambda k: project(around(x_, skip_two(k // 3)), around(z, skip_two(lax.rem(k, 3)))))

    for half in range(2):
        src = chunk(half, -1, 0)
        ag_wait(half, src, 0)
        ag(half, src, top, 2, ahead[half][0])
        ag(half, src, whole, 6, ahead[1 - half][0])
        ag(half, src, whole, 7, ahead[1 - half][1])
        src = chunk(half, 1, 0)
        ag_wait(half, src, 1)
        ag(half, src, bottom, 2, ahead[half][1])
        ag(half, src, whole, 9, ahead[1 - half][0])
        ag(half, src, whole, 10, ahead[1 - half][1])
    for half in range(2):
        p, c = parts[half], spot[half]
        rs(half, p.at[around(c, 1), hi], l2.at[half, hi], 2, ahead[half][0])
        rs(half, p.at[around(c, -1), lo], r2.at[half, lo], 3, ahead[half][1])

    homes = [home[0, retrieved[0, j // TOPK, j % TOPK]] for j in range(SLOTS)]
    owners = [h // PASS_DEV for h in homes]
    entries = []
    for j in range(SLOTS):
        rank = jnp.int32(0)
        for i in range(j):
            rank = rank + jnp.where(owners[i] == owners[j], 1, 0)
        entries.append(owners[j] * CAP + rank)
        ent[j] = entries[j]
    frequency = freq[...]
    sent, st = [out0, out1, out2], [st0, st1, st2]
    loads[5].wait()
    for c in range(CAP):
        row, slot, offset = jnp.int32(0), jnp.int32(0), jnp.int32(0)
        for j in range(SLOTS):
            hit = entries[j] == me * CAP + c
            row = jnp.where(hit, lax.rem(homes[j], PASS_DEV), row)
            slot = jnp.where(hit, j, slot)
            offset = jnp.where(hit, order[0, j // TOPK, j % TOPK] * PASS_LEN, offset)
        dropped = rec[0, pl.ds(slot, 1), :]
        ahead_of = (dropped - lax.broadcasted_iota(jnp.int32, (1, RECOMP), 1)).astype(F32)
        index = lax.broadcasted_iota(jnp.int32, (2 * HALF, RECOMP), 0).astype(F32)
        count = jnp.sum(jnp.where(ahead_of <= index, 1.0, 0.0), axis=1, keepdims=True)
        keep = index[:, :1] + count
        lanes = lax.broadcasted_iota(jnp.int32, (2 * HALF, PASS_LEN), 1).astype(F32)
        pick = jnp.where(lanes == keep, 1.0, 0.0).astype(BF16)
        cosine, sine = lane_tables(frequency * offset.astype(F32))

        def one_head(h):
            kept = jnp.dot(pick, storev[row, h], preferred_element_type=F32)
            keys = turned(kept[:, :HD], cosine, sine).astype(BF16)
            values = kept[:, HD:].astype(BF16)
            for half in range(2):
                for g in range(GROUPS):
                    start = half * HALF + STARTS[g]
                    to = sent[g].at[2 * h + half, c]
                    to[:, :HD] = keys[start : start + PIECES[g]]
                    to[:, HD:] = values[start : start + PIECES[g]]

        loop(KVH, one_head)

    for g in range(GROUPS):
        copy = pltpu.make_async_copy(
            sent[g].at[me], st[g].at[pl.ds(2 * me, CAP)], own_s.at[g]
        )
        copy.start()

    def passages(g):
        for dz, dx in STEPS:
            other = around(z, dz) * SIDE + around(x_, dx)
            to = st[g].at[pl.ds(2 * me, CAP)]
            remote(sent[g].at[other], to, st_s.at[g], st_r.at[g], (sec, other)).start()

    def passages_wait(g):
        pltpu.make_async_copy(
            sent[g].at[me], st[g].at[pl.ds(2 * me, CAP)], own_s.at[g]
        ).wait()
        arrived(st[g].at[pl.ds(0, CAP * (N_DEV - 1))], st_s.at[g], st_r.at[g])

    for half in range(2):
        src = chunk(half, 2, 0)
        ag_wait(half, src, 2)
        ag(half, src, whole, 12, ahead[1 - half][0])
        ag(half, src, whole, 13, ahead[1 - half][1])

    def second_axis(k, first):
        b = 3 + 3 * k
        for half in range(2):
            src = chunk(half, first, -1)
            ag_wait(half, src, b)
            ag(half, src, top, b + 2, ahead[1 - half][0])
            src = chunk(half, first, 1)
            ag_wait(half, src, b + 1)
            ag(half, src, bottom, b + 2, ahead[1 - half][1])

    second_axis(0, 0)

    for half in range(2):
        p, c = parts[half], spot[half]
        rs_arrived(half, l1.at[half], 0)
        block = p.at[around(c, 1), lo]
        block[...] = (block[...].astype(F32) + l1[half].astype(F32)).astype(BF16)
        rs(half, block, l2.at[half, lo], 2, ahead[half][0])
        rs_arrived(half, r1.at[half], 1)
        block = p.at[around(c, -1), hi]
        block[...] = (block[...].astype(F32) + r1[half].astype(F32)).astype(BF16)
        rs(half, block, r2.at[half, hi], 3, ahead[half][1])

    second_axis(1, -1)
    second_axis(2, 1)
    second_axis(3, 2)

    for half in range(2):
        p, c = parts[half], spot[half]
        rs_arrived(half, l2.at[half], 2)
        rs_arrived(half, r2.at[half], 3)
        for u in range(SIDE):
            block = p.at[c, u]
            total = block[...].astype(F32) + l2[half, u].astype(F32) + r2[half, u].astype(F32)
            block[...] = total.astype(BF16)
        far = around(spot[1 - half], 2)
        rs(half, p.at[c, far, upper], z1.at[half, upper], 4, ahead[1 - half][0])
        rs(half, p.at[c, far, lower], z1.at[half, lower], 5, ahead[1 - half][1])
    for half in range(2):
        p, c, d = parts[half], spot[half], spot[1 - half]
        for k, span in ((1, upper), (-1, lower)):
            rs_arrived(half, z1.at[half, span], 4 + (1 - k) // 2)
            block = p.at[c, around(d, k), span]
            block[...] = (block[...].astype(F32) + z1[half, span].astype(F32)).astype(BF16)
        rs(half, p.at[c, around(d, 1)], z2.at[half, 0], 6, ahead[1 - half][0])
        rs(half, p.at[c, around(d, -1)], z2.at[half, 1], 7, ahead[1 - half][1])
    passages(0)

    for k in (6, 7, 8):
        loads[k].wait()
    for half in range(2):
        for k in range(SIDE):
            ag_wait(half, chunk(half, (0, -1, 1, 2)[k], 2), 5 + 3 * k)

    def project_queries(k):
        span = pl.ds(pl.multiple_of(k * 2 * QLEN, 2 * QLEN), 2 * QLEN)
        weight = qv[span, :]
        for half in range(2):
            qacc[half] += jnp.dot(xall[half, k], weight, preferred_element_type=F32)

    qacc[...] = jnp.zeros_like(qacc)
    loop(N_DEV, project_queries)
    token_at = lax.broadcasted_iota(jnp.int32, (QLEN, 1), 0) + TOPK * PASS_LEN
    token_angles = token_at.astype(F32) * frequency
    cosine, sine = lane_tables(token_angles)
    base = 2 * mine
    for half in range(2):
        for j in range(2):
            head = turned(qacc[half, :, j * HD : (j + 1) * HD], cosine, sine)
            q4[half, base + j] = head.astype(BF16)

    def share_queries(r):
        block = q4.at[r, pl.ds(base, 2)]
        push(sends, block, block, q_s.at[r], q_r.at[r], pair)

    share_queries(0)

    for g in range(1, GROUPS):
        passages(g)
    share_queries(1)

    slot_at = lax.broadcasted_iota(jnp.int32, (SLOTS, 1), 0)
    offsets = jnp.zeros((SLOTS, 1), jnp.int32)
    for j in range(SLOTS):
        offsets = jnp.where(slot_at == j, order[0, j // TOPK, j % TOPK] * PASS_LEN, offsets)
    places = rec[0] + offsets
    angle[pl.ds(0, QLEN)] = token_angles
    for i in range(FRESH):
        here = places[:, i : i + 1]
        if FRESH + i < RECOMP:
            here = jnp.where(mine == 0, here, places[:, FRESH + i : FRESH + i + 1])
        angle[pl.ds(QLEN + i * SLOTS, SLOTS)] = here.astype(F32) * frequency
    cosine, sine = lane_tables(angle[...])
    for half in range(2):
        p, c = parts[half], spot[half]
        total = p[c, spot[1 - half]].astype(F32)
        for k in range(2):
            rs_arrived(half, z2.at[half, k], 6 + k)
            total += z2[half, k].astype(F32)
        total = total.astype(BF16).astype(F32)
        if half == 0:
            total = turned(total, cosine, sine)
        own_to, fresh_to = (ko, kf) if half == 0 else (vo, vf)
        own_to[...] = total[:QLEN].astype(BF16)
        fresh = total[QLEN:].reshape(FRESH, SLOTS, HD)
        for r in range(REQ_SECTION):
            rows_of = fresh[:, r * TOPK : (r + 1) * TOPK].reshape(FRESH * TOPK, HD)
            filler = jnp.zeros((FROWS - FRESH * TOPK, HD), F32)
            fresh_to[r] = jnp.concatenate([rows_of, filler], axis=0).astype(BF16)

    cols = 4 * QLEN

    def score(keys, queries):
        s = lax.dot_general(
            keys, queries, (((1,), (1,)), ((), ())), preferred_element_type=F32
        )
        return s * SCALE

    def update(r, scores, values):
        old = m[r]
        new = old
        for s in scores:
            new = jnp.maximum(new, jnp.max(s, axis=0, keepdims=True))
        scale = jnp.exp2(old - new)
        total, mixed = l[r] * scale, acc[r] * scale
        for s, v in zip(scores, values):
            weights = jnp.exp2(s - new)
            total = total + jnp.sum(weights, axis=0, keepdims=True)
            mixed = mixed + lax.dot_general(
                v, weights.astype(BF16), (((0,), (0,)), ((), ())), preferred_element_type=F32
            )
        m[r], l[r], acc[r] = new, total, mixed

    def bias(count, valid):
        index = lax.broadcasted_iota(jnp.int32, (count, 1), 0)
        return jnp.where(index < valid, 0.0, -jnp.inf)

    def queries_of(r):
        return q4[r].reshape(cols, HD)

    def stored(r, g):
        many = 2 if g == 0 else 4

        def some(k):
            scores, values = [], []
            for i in range(many):
                e = ent[r * TOPK + many * k + i]
                block = st[g].at[e]
                s = score(block[:, :HD], queries_of(r))
                if g == GROUPS - 1:
                    s = s + bias(PIECES[g], PIECES[g] - (2 * HALF - KEPT) * mine)
                scores.append(s)
                values.append(block[:, HD:])
            update(r, scores, values)

        loop(TOPK // many, some)

    def computed(r):
        block = q4.at[r, pl.ds(2 - base, 2)]
        arrived(block, q_s.at[r], q_r.at[r])
        s = score(kf[r], queries_of(r)) + bias(FROWS, FRESH * TOPK - TOPK * mine)
        update(r, [s], [vf[r]])

        @pl.when(mine == r)
        def _():
            s = score(ko[...], queries_of(r))
            keys_at = lax.broadcasted_iota(jnp.int32, (QLEN, cols), 0)
            query_at = lax.rem(lax.broadcasted_iota(jnp.int32, (QLEN, cols), 1), QLEN)
            s = jnp.where(keys_at <= query_at, s, -jnp.inf)
            update(r, [s], [vo[...]])

    m[...] = jnp.full_like(m, -1e30)
    l[...] = jnp.zeros_like(l)
    acc[...] = jnp.zeros_like(acc)
    per = BLOCKS // REQ_SECTION

    size = REQ_SECTION * QLEN // BLOCKS

    def finish(r):
        done = (acc[r] / l[r]).astype(BF16)
        level = m[r] + jnp.log2(l[r])
        for j in range(4):
            span = slice(j * QLEN, (j + 1) * QLEN)
            oall[r, j // 2, pl.ds((j % 2) * HD, HD), :] = done[:, span]
            lall[r, j // 2, pl.ds(j % 2, 1), :] = level[:, span]
        sem = (1 + per) * r
        push(sends, lall.at[r, 1 - mine], lin.at[r], ex_s.at[sem], ex_r.at[sem], pair)
        for k in range(per):
            span = pl.ds(k * size, size)
            push(sends, oall.at[r, 1 - mine, :, span], oin.at[r, :, span],
                 ex_s.at[sem + 1 + k], ex_r.at[sem + 1 + k], pair)

    def join(b):
        r, k = b // per, b % per
        sem = (1 + per) * r
        if k == 0:
            arrived(lin.at[r], ex_s.at[sem], ex_r.at[sem])
        here = pl.ds(k * size, size)
        arrived(oin.at[r, :, here], ex_s.at[sem + 1 + k], ex_r.at[sem + 1 + k])
        for j in range(2):
            a, b_ = lall[r, mine, pl.ds(j, 1), here], lin[r, pl.ds(j, 1), here]
            most = jnp.maximum(a, b_)
            a, b_ = jnp.exp2(a - most), jnp.exp2(b_ - most)
            span = pl.ds(j * HD, HD)
            joined = oall[r, mine, span, here].astype(F32) * a
            joined = (joined + oin[r, span, here].astype(F32) * b_) / (a + b_)
            att[b * size : (b + 1) * size, j * HD : (j + 1) * HD] = joined.T.astype(BF16)

    part = size // 2
    width = xall.shape[3]

    def units(b, half, first, second, count):
        return xall.at[half, pl.ds(first * SIDE + second, count), pl.ds(b * part, part)]

    def compute(blocks, xx, zz):
        span = pl.ds(pl.multiple_of((zz * SIDE + xx) * width, width), width)
        from_row, to_row = blocks[0] * size, (blocks[-1] + 1) * size
        got = jnp.dot(
            att[from_row:to_row, :], wv[:, span], preferred_element_type=F32
        ).astype(BF16)
        for k, b in enumerate(blocks):
            here = pl.ds(b * part, part)
            xall[0, xx * SIDE + zz, here] = got[k * size : k * size + part]
            xall[1, zz * SIDE + xx, here] = got[k * size + part : (k + 1) * size]

    def out_push(b, half, sem, src, dst, target):
        s = 2 * b + half
        remote(src, dst, br_s.at[s], br_r.at[5 * s + sem], target).start()

    def out_arrived(b, half, sem, block):
        s = 2 * b + half
        arrived(block, br_s.at[s], br_r.at[5 * s + sem])

    def first(blocks):
        loop(SIDE, lambda k: compute(blocks, around(x_, 2), around(z, k)))
        loop(SIDE - 1, lambda k: compute(blocks, around(x_, skip_two(k)), around(z, 2)))
        for b in blocks:
            for half in range(2):
                c, to, back = spot[half], *ahead[half]
                out_push(b, half, 0, units(b, half, around(c, 2), 0, 2), bl1.at[b, half], to)
                out_push(b, half, 1, units(b, half, around(c, 2), 2, 2), br1.at[b, half], back)
        loop(
            9,
            lambda k: compute(
                blocks, around(x_, skip_two(k // 3)), around(z, skip_two(lax.rem(k, 3)))
            ),
        )
        for b in blocks:
            for half in range(2):
                c, to, back = spot[half], *ahead[half]
                out_push(b, half, 2, units(b, half, around(c, 1), 2, 2), bl2.at[b, half, hi], to)
                out_push(b, half, 3, units(b, half, around(c, -1), 0, 2), br2.at[b, half, lo], back)

    def second(b):
        for half in range(2):
            c = spot[half]
            out_arrived(b, half, 0, bl1.at[b, half])
            block = units(b, half, around(c, 1), 0, 2)
            block[...] = (block[...].astype(F32) + bl1[b, half].astype(F32)).astype(BF16)
            out_push(b, half, 2, block, bl2.at[b, half, lo], ahead[half][0])
            out_arrived(b, half, 1, br1.at[b, half])
            block = units(b, half, around(c, -1), 2, 2)
            block[...] = (block[...].astype(F32) + br1[b, half].astype(F32)).astype(BF16)
            out_push(b, half, 3, block, br2.at[b, half, hi], ahead[half][1])

    def third(b):
        for half in range(2):
            c = spot[half]
            out_arrived(b, half, 2, bl2.at[b, half])
            out_arrived(b, half, 3, br2.at[b, half])
            block = units(b, half, c, 0, SIDE)
            total = block[...].astype(F32) + bl2[b, half].astype(F32) + br2[b, half].astype(F32)
            block[...] = total.astype(BF16)
            for k in (1, 3, 2, 0):
                other = around(spot[1 - half], k)
                target = (after, other * SIDE + x_) if half == 0 else (after, z * SIDE + other)
                src = xall.at[half, c * SIDE + other, pl.ds(b * part, part)]
                out_push(b, half, 4, src, bz2.at[b, half, k], target)

    results = []

    def fourth(b):
        if b > 1:
            results[b - 2].wait()
        for half in range(2):
            out_arrived(b, half, 4, bz2.at[b, half])
            total = bz2[b, half, 0].astype(F32)
            for k in range(1, SIDE):
                total += bz2[b, half, k].astype(F32)
            outv[b % 2, pl.ds(half * part, part), :] = total
        to = out.at[pl.ds(b * size, size)]
        results.append(pltpu.make_async_copy(outv.at[b % 2], to, loc.at[10 + b]))
        results[b].start()

    computed(0)
    for g in range(GROUPS):
        passages_wait(g)
        stored(0, g)
    finish(0)
    for half in range(2):
        gone = xall.at[half, pl.ds(0, N_DEV - 1)]
        remote(gone, gone, ag_s.at[half], ag_r.at[0], right).wait_send()
    loads[9].wait()
    for group in FIRSTS:
        for b in group:
            join(b)
        first(group)
    computed(1)
    stored(1, 0)
    second(0)
    second(1)
    for g in range(1, GROUPS):
        stored(1, g)
    finish(1)
    third(0)
    join(2)
    first((2,))
    third(1)
    join(3)
    first((3,))
    second(2)
    second(3)
    third(2)
    third(3)
    for b in range(BLOCKS):
        fourth(b)
    for copy in sends:
        copy.wait_send()

    def gone(block, sem):
        remote(block, block, sem, br_r.at[0], right).wait_send()

    for half in range(2):
        gone(parts[half].at[pl.ds(0, SIDE - 1)], rs_s.at[2 * half])
        gone(parts[half].at[0, pl.ds(0, SIDE - 1)], rs_s.at[2 * half + 1])
        for b in range(BLOCKS):
            gone(units(b, half, 0, 0, N_DEV), br_s.at[2 * b + half])
    for g in range(GROUPS):
        gone(sent[g].at[pl.ds(0, N_DEV - 1)], st_s.at[g])
    for copy in results[-2:]:
        copy.wait()


def layer(home, retrieved, order, x, hid, kvw, qw, ow, store, rec, freq):
    anywhere = pl.BlockSpec(memory_space=pl.ANY)
    vmem = pl.BlockSpec(memory_space=pltpu.VMEM)
    smem = pl.BlockSpec(memory_space=pltpu.SMEM)
    dma = pltpu.SemaphoreType.DMA
    d_here = x.shape[1]
    cols = 4 * QLEN
    part = REQ_SECTION * QLEN // BLOCKS // 2
    width = ow.shape[1] // N_DEV
    assert width == d_here

    def bf16(*shape):
        return pltpu.VMEM(shape, BF16)

    def f32(*shape):
        return pltpu.VMEM(shape, F32)

    return pl.pallas_call(
        layer_kernel,
        out_shape=jax.ShapeDtypeStruct((REQ_SECTION * QLEN, width), F32),
        in_specs=[smem] * 3 + [anywhere] * 6 + [vmem] * 2,
        out_specs=anywhere,
        scratch_shapes=[
            pltpu.SMEM((SLOTS,), jnp.int32),
            bf16(2, N_DEV, QLEN, d_here),
            bf16(*qw.shape),
            bf16(*kvw.shape),
            bf16(REQ_SECTION, GROUP, d_here),
            bf16(SIDE, SIDE, GROUP, HD),
            bf16(SIDE, SIDE, GROUP, HD),
            bf16(2, 2, GROUP, HD),
            bf16(2, 2, GROUP, HD),
            bf16(2, SIDE, GROUP, HD),
            bf16(2, SIDE, GROUP, HD),
            bf16(2, GROUP, HD),
            bf16(2, 2, GROUP, HD),
            f32(2, QLEN, 2 * HD),
            bf16(*store.shape),
            *[bf16(N_DEV, CAP, piece, 2 * HD) for piece in PIECES],
            *[bf16(N_DEV * CAP, piece, 2 * HD) for piece in PIECES],
            bf16(REQ_SECTION, 4, QLEN, HD),
            bf16(REQ_SECTION, FROWS, HD),
            bf16(REQ_SECTION, FROWS, HD),
            bf16(QLEN, HD),
            bf16(QLEN, HD),
            f32(REQ_SECTION, HD, cols),
            f32(REQ_SECTION, 1, cols),
            f32(REQ_SECTION, 1, cols),
            f32(GROUP, HD),
            bf16(REQ_SECTION, 2, 2 * HD, QLEN),
            f32(REQ_SECTION, 2, 8, QLEN),
            bf16(REQ_SECTION, 2 * HD, QLEN),
            f32(REQ_SECTION, 8, QLEN),
            bf16(*ow.shape),
            bf16(REQ_SECTION * QLEN, 2 * HD),
            bf16(BLOCKS, 2, 2, part, width),
            bf16(BLOCKS, 2, 2, part, width),
            bf16(BLOCKS, 2, SIDE, part, width),
            bf16(BLOCKS, 2, SIDE, part, width),
            bf16(BLOCKS, 2, SIDE, part, width),
            f32(2, 2 * part, width),
            dma((10 + BLOCKS,)),
            dma((GROUPS,)),
            dma((2,)),
            dma((30,)),
            dma((4,)),
            dma((16,)),
            dma((GROUPS,)),
            dma((GROUPS,)),
            dma((2,)),
            dma((2,)),
            dma((2 + BLOCKS,)),
            dma((2 + BLOCKS,)),
            dma((2 * BLOCKS,)),
            dma((10 * BLOCKS,)),
        ],
        compiler_params=pltpu.CompilerParams(
            collective_id=0, has_side_effects=True, vmem_limit_bytes=63 * 2**20
        ),
        name="layer",
    )(home, retrieved, order, x, hid, kvw, qw, ow, store, rec, freq)


def body(
    activations, q_weight, out_weight, kv_weight, passage_store,
    passage_home, retrieved, slot_order, recomputed, passage_hidden,
):
    exponents = -np.arange(HD // 2, dtype=np.float32) * np.float32(2.0 / HD)
    frequency = np.float32(ROPE_BASE) ** exponents
    frequency = jnp.asarray(np.concatenate([frequency, frequency])[None])
    hidden = passage_hidden[0].transpose(1, 0, 2).reshape(RECOMP * SLOTS, -1)
    out = layer(
        passage_home, retrieved, slot_order, activations[0], hidden, kv_weight[0], q_weight[0],
        out_weight[0], passage_store[0], recomputed, frequency,
    )
    return out.astype(BF16)[None]


def solution(mesh):
    in_specs = (
        P("section", None, "dev"),
        P("section", None, "dev"),
        P("section", "dev", None),
        P("section", "dev", None),
        P("section", "dev", None, None, None),
        P("section", None),
        P("section", None, None),
        P("section", None, None),
        P("section", None, None),
        P("section", None, None, "dev"),
    )
    out_specs = P("section", None, "dev")
    return jax.shard_map(body, mesh=mesh, in_specs=in_specs, out_specs=out_specs, check_vma=False)
```

```python
import functools

import jax
import jax.numpy as jnp
import numpy as np
from jax import lax
from jax.experimental import pallas as pl
from jax.experimental.pallas import tpu as pltpu
from jax.sharding import PartitionSpec as P

QH = 32
KVH = 8
HD = 128
PASS_LEN = 512
TOPK = 8
RECOMP = 77
REQ_SECTION = 2
QLEN = 256
SLOTS = 16
CAP = 2
PASS_DEV = 4
SIDE = 4
N_DEV = 16
FRESH = 39
GROUP = QLEN + FRESH * SLOTS
FROWS = 320
KEPT = PASS_LEN - RECOMP
HALF = 224
PIECES = (128, 64, 32)
STARTS = (0, 128, 192)
GROUPS = len(PIECES)
BLOCKS = 4
FIRSTS = ((0,), (1,))
ROPE_BASE = 500000.0
MESH = pl.DeviceIdType.MESH
F32 = jnp.float32
BF16 = jnp.bfloat16
SCALE = HD**-0.5 * 1.4426950408889634


def lane_tables(angles):
    sign = jnp.where(lax.broadcasted_iota(jnp.int32, (1, HD), 1) < HD // 2, -1.0, 1.0)
    return jnp.cos(angles), jnp.sin(angles) * sign


def turned(v, cosine, sine):
    return v * cosine + pltpu.roll(v, HD // 2, axis=1) * sine


def place():
    d = lax.axis_index("dev")
    return lax.axis_index("section"), d // SIDE, lax.rem(d, SIDE)


def around(v, step):
    return lax.rem(v + step + SIDE, SIDE)


def remote(src, dst, send, recv, target):
    return pltpu.make_async_remote_copy(
        src_ref=src,
        dst_ref=dst,
        send_sem=send,
        recv_sem=recv,
        device_id=target,
        device_id_type=MESH,
    )


STEPS = (
    (1, 1), (3, 3), (0, 2), (1, 3), (3, 1), (2, 0), (2, 1), (0, 3),
    (3, 2), (1, 0), (2, 3), (0, 1), (1, 2), (3, 0), (2, 2),
)


def layer_kernel(
    home, retrieved, order, x, hid, kvw, qw, ow, store, rec, freq, out,
    ent, xall, qv, kvv, rows, pa, pb, l1, r1, l2, r2, z1, z2, qacc,
    storev, out0, out1, out2, st0, st1, st2, q4, kf, vf, ko, vo, acc, m, l,
    angle, oall, lall, oin, lin, wv, att, bl1, br1, bl2, br2, bz2, outv,
    loc, own_s, ag_s, ag_r, rs_s, rs_r, st_s, st_r, q_s, q_r, ex_s, ex_r, br_s, br_r, ready,
):
    sec = lax.axis_index("section")
    me = lax.axis_index("dev")
    z, x_ = me // SIDE, lax.rem(me, SIDE)
    sections = lax.axis_size("section")
    after, before = lax.rem(sec + 1, sections), lax.rem(sec + sections - 1, sections)
    mine = lax.rem(me, 2)

    def at(zz, xx):
        return (sec, zz * SIDE + xx)

    right, left = at(z, around(x_, 1)), at(z, around(x_, -1))
    down, up = at(around(z, 1), x_), at(around(z, -1), x_)
    pair = (sec, me + 1 - 2 * mine)
    ahead = [(right, left), (down, up)]
    spot = [x_, z]

    greeted = [right, left, down, up, (after, me), (before, me)]
    barrier = pltpu.get_barrier_semaphore()
    for target in greeted:
        pl.semaphore_signal(barrier, inc=1, device_id=target, device_id_type=MESH)

    first_rows, last_rows = FRESH * SLOTS, (RECOMP - FRESH) * SLOTS
    loads = [
        pltpu.make_async_copy(kvw, kvv, loc.at[0]),
        pltpu.make_async_copy(x.at[pl.ds(0, QLEN)], rows.at[0, pl.ds(0, QLEN)], loc.at[1]),
        pltpu.make_async_copy(x.at[pl.ds(QLEN, QLEN)], rows.at[1, pl.ds(0, QLEN)], loc.at[2]),
        pltpu.make_async_copy(
            hid.at[pl.ds(0, first_rows)], rows.at[0, pl.ds(QLEN, first_rows)], loc.at[3]
        ),
        pltpu.make_async_copy(
            hid.at[pl.ds(first_rows, last_rows)], rows.at[1, pl.ds(QLEN, last_rows)], loc.at[4]
        ),
        pltpu.make_async_copy(store, storev, loc.at[5]),
        pltpu.make_async_copy(qw, qv, loc.at[6]),
        pltpu.make_async_copy(x.at[pl.ds(0, QLEN)], xall.at[0, me], loc.at[7]),
        pltpu.make_async_copy(x.at[pl.ds(QLEN, QLEN)], xall.at[1, me], loc.at[8]),
        pltpu.make_async_copy(ow, wv, loc.at[9]),
    ]
    for load in loads:
        load.start()
    rest = rows.at[1, pl.ds(QLEN + last_rows, GROUP - QLEN - last_rows)]
    rest[...] = jnp.zeros_like(rest)
    pl.semaphore_wait(barrier, len(greeted))

    def chunk(half, first, second):
        if half == 0:
            return around(z, second) * SIDE + around(x_, first)
        return around(z, first) * SIDE + around(x_, second)

    top, bottom = pl.ds(0, QLEN // 2), pl.ds(QLEN // 2, QLEN // 2)
    whole = pl.ds(0, QLEN)
    sends = []

    def ag(half, src, span, sem, target, own=False):
        to = xall.at[half, src, span]
        frm = x.at[pl.ds(half * QLEN, QLEN)] if own else to
        remote(frm, to, ag_s.at[half], ag_r.at[15 * half + sem], target).start()

    def ag_wait(half, src, sem):
        to = xall.at[half, src, whole]
        remote(to, to, ag_s.at[half], ag_r.at[15 * half + sem], right).wait_recv()

    for half in range(2):
        ag(half, me, whole, 0, ahead[half][0], True)
        ag(half, me, whole, 1, ahead[half][1], True)
    for half in range(2):
        ag(half, me, whole, 3, ahead[1 - half][0], True)
        ag(half, me, whole, 4, ahead[1 - half][1], True)

    def push(group, src, dst, send, recv, target):
        copy = remote(src, dst, send, recv, target)
        copy.start()
        group.append(copy)

    def arrived(block, send, recv):
        remote(block, block, send, recv, right).wait_recv()

    def project(xx, zz):
        head = 2 * zz + xx // 2
        span = pl.ds(pl.multiple_of(head * 2 * HD, 2 * HD), 2 * HD)
        part = jnp.dot(rows[lax.rem(xx, 2)], kvv[:, span], preferred_element_type=F32)
        part = part.astype(BF16)
        pa[xx, zz] = part[:, :HD]
        pb[zz, xx] = part[:, HD:]

    def loop(count, step):
        def one(k, carry):
            step(k)
            return carry

        lax.fori_loop(0, count, one, 0)

    def skip_two(t):
        return t + t // 2

    parts = [pa, pb]
    lo, hi = pl.ds(0, 2), pl.ds(2, 2)

    def rs(half, src, dst, sem, target):
        remote(src, dst, rs_s.at[2 * half + sem // 4], rs_r.at[8 * half + sem], target).start()

    def rs_arrived(half, block, sem):
        arrived(block, rs_s.at[2 * half + sem // 4], rs_r.at[8 * half + sem])

    upper, lower = pl.ds(0, GROUP // 32 * 16), pl.ds(GROUP // 32 * 16, GROUP - GROUP // 32 * 16)

    def rs_first(half):
        p, c = parts[half], spot[half]
        rs(half, p.at[around(c, 2), lo], l1.at[half], 0, ahead[half][0])
        rs(half, p.at[around(c, 2), hi], r1.at[half], 1, ahead[half][1])

    for k in range(5):
        loads[k].wait()
    loop(SIDE, lambda k: project(around(x_, 2), around(z, k)))
    rs_first(0)
    loop(SIDE - 1, lambda k: project(around(x_, skip_two(k)), around(z, 2)))
    rs_first(1)
    loop(9, lambda k: project(around(x_, skip_two(k // 3)), around(z, skip_two(lax.rem(k, 3)))))

    for half in range(2):
        src = chunk(half, -1, 0)
        ag_wait(half, src, 0)
        ag(half, src, top, 2, ahead[half][0])
        ag(half, src, whole, 6, ahead[1 - half][0])
        ag(half, src, whole, 7, ahead[1 - half][1])
        src = chunk(half, 1, 0)
        ag_wait(half, src, 1)
        ag(half, src, bottom, 2, ahead[half][1])
        ag(half, src, whole, 9, ahead[1 - half][0])
        ag(half, src, whole, 10, ahead[1 - half][1])
    for half in range(2):
        p, c = parts[half], spot[half]
        rs(half, p.at[around(c, 1), hi], l2.at[half, hi], 2, ahead[half][0])
        rs(half, p.at[around(c, -1), lo], r2.at[half, lo], 3, ahead[half][1])

    homes = [home[0, retrieved[0, j // TOPK, j % TOPK]] for j in range(SLOTS)]
    owners = [h // PASS_DEV for h in homes]
    entries = []
    for j in range(SLOTS):
        rank = jnp.int32(0)
        for i in range(j):
            rank = rank + jnp.where(owners[i] == owners[j], 1, 0)
        entries.append(owners[j] * CAP + rank)
        ent[j] = entries[j]
    frequency = freq[...]
    sent, st = [out0, out1, out2], [st0, st1, st2]
    loads[5].wait()
    for c in range(CAP):
        row, slot, offset = jnp.int32(0), jnp.int32(0), jnp.int32(0)
        for j in range(SLOTS):
            hit = entries[j] == me * CAP + c
            row = jnp.where(hit, lax.rem(homes[j], PASS_DEV), row)
            slot = jnp.where(hit, j, slot)
            offset = jnp.where(hit, order[0, j // TOPK, j % TOPK] * PASS_LEN, offset)
        dropped = rec[0, pl.ds(slot, 1), :]
        ahead_of = (dropped - lax.broadcasted_iota(jnp.int32, (1, RECOMP), 1)).astype(F32)
        index = lax.broadcasted_iota(jnp.int32, (2 * HALF, RECOMP), 0).astype(F32)
        count = jnp.sum(jnp.where(ahead_of <= index, 1.0, 0.0), axis=1, keepdims=True)
        keep = index[:, :1] + count
        lanes = lax.broadcasted_iota(jnp.int32, (2 * HALF, PASS_LEN), 1).astype(F32)
        pick = jnp.where(lanes == keep, 1.0, 0.0).astype(BF16)
        cosine, sine = lane_tables(frequency * offset.astype(F32))

        def one_head(h):
            kept = jnp.dot(pick, storev[row, h], preferred_element_type=F32)
            keys = turned(kept[:, :HD], cosine, sine).astype(BF16)
            values = kept[:, HD:].astype(BF16)
            for half in range(2):
                for g in range(GROUPS):
                    start = half * HALF + STARTS[g]
                    to = sent[g].at[2 * h + half, c]
                    to[:, :HD] = keys[start : start + PIECES[g]]
                    to[:, HD:] = values[start : start + PIECES[g]]

        loop(KVH, one_head)

    for g in range(GROUPS):
        copy = pltpu.make_async_copy(
            sent[g].at[me], st[g].at[pl.ds(2 * me, CAP)], own_s.at[g]
        )
        copy.start()

    def passages(g):
        for dz, dx in STEPS:
            other = around(z, dz) * SIDE + around(x_, dx)
            to = st[g].at[pl.ds(2 * me, CAP)]
            remote(sent[g].at[other], to, st_s.at[g], st_r.at[g], (sec, other)).start()

    def passages_wait(g):
        pltpu.make_async_copy(
            sent[g].at[me], st[g].at[pl.ds(2 * me, CAP)], own_s.at[g]
        ).wait()
        arrived(st[g].at[pl.ds(0, CAP * (N_DEV - 1))], st_s.at[g], st_r.at[g])

    for half in range(2):
        src = chunk(half, 2, 0)
        ag_wait(half, src, 2)
        ag(half, src, whole, 12, ahead[1 - half][0])
        ag(half, src, whole, 13, ahead[1 - half][1])

    def second_axis(k, first):
        b = 3 + 3 * k
        for half in range(2):
            src = chunk(half, first, -1)
            ag_wait(half, src, b)
            ag(half, src, top, b + 2, ahead[1 - half][0])
            src = chunk(half, first, 1)
            ag_wait(half, src, b + 1)
            ag(half, src, bottom, b + 2, ahead[1 - half][1])

    second_axis(0, 0)

    for half in range(2):
        p, c = parts[half], spot[half]
        rs_arrived(half, l1.at[half], 0)
        block = p.at[around(c, 1), lo]
        block[...] = (block[...].astype(F32) + l1[half].astype(F32)).astype(BF16)
        rs(half, block, l2.at[half, lo], 2, ahead[half][0])
        rs_arrived(half, r1.at[half], 1)
        block = p.at[around(c, -1), hi]
        block[...] = (block[...].astype(F32) + r1[half].astype(F32)).astype(BF16)
        rs(half, block, r2.at[half, hi], 3, ahead[half][1])

    second_axis(1, -1)
    second_axis(2, 1)
    second_axis(3, 2)

    for half in range(2):
        p, c = parts[half], spot[half]
        rs_arrived(half, l2.at[half], 2)
        rs_arrived(half, r2.at[half], 3)
        for u in range(SIDE):
            block = p.at[c, u]
            total = block[...].astype(F32) + l2[half, u].astype(F32) + r2[half, u].astype(F32)
            block[...] = total.astype(BF16)
        far = around(spot[1 - half], 2)
        rs(half, p.at[c, far, upper], z1.at[half, upper], 4, ahead[1 - half][0])
        rs(half, p.at[c, far, lower], z1.at[half, lower], 5, ahead[1 - half][1])
    for half in range(2):
        p, c, d = parts[half], spot[half], spot[1 - half]
        for k, span in ((1, upper), (-1, lower)):
            rs_arrived(half, z1.at[half, span], 4 + (1 - k) // 2)
            block = p.at[c, around(d, k), span]
            block[...] = (block[...].astype(F32) + z1[half, span].astype(F32)).astype(BF16)
        rs(half, p.at[c, around(d, 1)], z2.at[half, 0], 6, ahead[1 - half][0])
        rs(half, p.at[c, around(d, -1)], z2.at[half, 1], 7, ahead[1 - half][1])

    for k in (6, 7, 8):
        loads[k].wait()
    for half in range(2):
        for k in range(SIDE):
            ag_wait(half, chunk(half, (0, -1, 1, 2)[k], 2), 5 + 3 * k)
    pl.semaphore_signal(ready, inc=1, device_id=(before, me), device_id_type=MESH)
    passages(0)

    def project_queries(k):
        span = pl.ds(pl.multiple_of(k * 2 * QLEN, 2 * QLEN), 2 * QLEN)
        weight = qv[span, :]
        for half in range(2):
            qacc[half] += jnp.dot(xall[half, k], weight, preferred_element_type=F32)

    qacc[...] = jnp.zeros_like(qacc)
    loop(N_DEV, project_queries)
    token_at = lax.broadcasted_iota(jnp.int32, (QLEN, 1), 0) + TOPK * PASS_LEN
    token_angles = token_at.astype(F32) * frequency
    cosine, sine = lane_tables(token_angles)
    base = 2 * mine
    for half in range(2):
        for j in range(2):
            head = turned(qacc[half, :, j * HD : (j + 1) * HD], cosine, sine)
            q4[half, base + j] = head.astype(BF16)

    def share_queries(r):
        block = q4.at[r, pl.ds(base, 2)]
        push(sends, block, block, q_s.at[r], q_r.at[r], pair)

    share_queries(0)

    for g in range(1, GROUPS):
        passages(g)
    share_queries(1)

    slot_at = lax.broadcasted_iota(jnp.int32, (SLOTS, 1), 0)
    offsets = jnp.zeros((SLOTS, 1), jnp.int32)
    for j in range(SLOTS):
        offsets = jnp.where(slot_at == j, order[0, j // TOPK, j % TOPK] * PASS_LEN, offsets)
    places = rec[0] + offsets
    angle[pl.ds(0, QLEN)] = token_angles
    for i in range(FRESH):
        here = places[:, i : i + 1]
        if FRESH + i < RECOMP:
            here = jnp.where(mine == 0, here, places[:, FRESH + i : FRESH + i + 1])
        angle[pl.ds(QLEN + i * SLOTS, SLOTS)] = here.astype(F32) * frequency
    cosine, sine = lane_tables(angle[...])
    for half in range(2):
        p, c = parts[half], spot[half]
        total = p[c, spot[1 - half]].astype(F32)
        for k in range(2):
            rs_arrived(half, z2.at[half, k], 6 + k)
            total += z2[half, k].astype(F32)
        total = total.astype(BF16).astype(F32)
        if half == 0:
            total = turned(total, cosine, sine)
        own_to, fresh_to = (ko, kf) if half == 0 else (vo, vf)
        own_to[...] = total[:QLEN].astype(BF16)
        fresh = total[QLEN:].reshape(FRESH, SLOTS, HD)
        for r in range(REQ_SECTION):
            rows_of = fresh[:, r * TOPK : (r + 1) * TOPK].reshape(FRESH * TOPK, HD)
            filler = jnp.zeros((FROWS - FRESH * TOPK, HD), F32)
            fresh_to[r] = jnp.concatenate([rows_of, filler], axis=0).astype(BF16)

    cols = 4 * QLEN

    def score(keys, queries):
        s = lax.dot_general(
            keys, queries, (((1,), (1,)), ((), ())), preferred_element_type=F32
        )
        return s * SCALE

    def update(r, scores, values):
        old = m[r]
        new = old
        for s in scores:
            new = jnp.maximum(new, jnp.max(s, axis=0, keepdims=True))
        scale = jnp.exp2(old - new)
        total, mixed = l[r] * scale, acc[r] * scale
        for s, v in zip(scores, values):
            weights = jnp.exp2(s - new)
            total = total + jnp.sum(weights, axis=0, keepdims=True)
            mixed = mixed + lax.dot_general(
                v, weights.astype(BF16), (((0,), (0,)), ((), ())), preferred_element_type=F32
            )
        m[r], l[r], acc[r] = new, total, mixed

    def bias(count, valid):
        index = lax.broadcasted_iota(jnp.int32, (count, 1), 0)
        return jnp.where(index < valid, 0.0, -jnp.inf)

    def queries_of(r):
        return q4[r].reshape(cols, HD)

    def stored(r, g):
        many = 2 if g == 0 else 4

        def some(k):
            scores, values = [], []
            for i in range(many):
                e = ent[r * TOPK + many * k + i]
                block = st[g].at[e]
                s = score(block[:, :HD], queries_of(r))
                if g == GROUPS - 1:
                    s = s + bias(PIECES[g], PIECES[g] - (2 * HALF - KEPT) * mine)
                scores.append(s)
                values.append(block[:, HD:])
            update(r, scores, values)

        loop(TOPK // many, some)

    def computed(r):
        block = q4.at[r, pl.ds(2 - base, 2)]
        arrived(block, q_s.at[r], q_r.at[r])
        s = score(kf[r], queries_of(r)) + bias(FROWS, FRESH * TOPK - TOPK * mine)
        update(r, [s], [vf[r]])

        @pl.when(mine == r)
        def _():
            s = score(ko[...], queries_of(r))
            keys_at = lax.broadcasted_iota(jnp.int32, (QLEN, cols), 0)
            query_at = lax.rem(lax.broadcasted_iota(jnp.int32, (QLEN, cols), 1), QLEN)
            s = jnp.where(keys_at <= query_at, s, -jnp.inf)
            update(r, [s], [vo[...]])

    m[...] = jnp.full_like(m, -1e30)
    l[...] = jnp.zeros_like(l)
    acc[...] = jnp.zeros_like(acc)
    per = BLOCKS // REQ_SECTION

    size = REQ_SECTION * QLEN // BLOCKS

    def finish(r):
        done = (acc[r] / l[r]).astype(BF16)
        level = m[r] + jnp.log2(l[r])
        for j in range(4):
            span = slice(j * QLEN, (j + 1) * QLEN)
            oall[r, j // 2, pl.ds((j % 2) * HD, HD), :] = done[:, span]
            lall[r, j // 2, pl.ds(j % 2, 1), :] = level[:, span]
        sem = (1 + per) * r
        push(sends, lall.at[r, 1 - mine], lin.at[r], ex_s.at[sem], ex_r.at[sem], pair)
        for k in range(per):
            span = pl.ds(k * size, size)
            push(sends, oall.at[r, 1 - mine, :, span], oin.at[r, :, span],
                 ex_s.at[sem + 1 + k], ex_r.at[sem + 1 + k], pair)

    def join(b):
        r, k = b // per, b % per
        sem = (1 + per) * r
        if k == 0:
            arrived(lin.at[r], ex_s.at[sem], ex_r.at[sem])
        here = pl.ds(k * size, size)
        arrived(oin.at[r, :, here], ex_s.at[sem + 1 + k], ex_r.at[sem + 1 + k])
        for j in range(2):
            a, b_ = lall[r, mine, pl.ds(j, 1), here], lin[r, pl.ds(j, 1), here]
            most = jnp.maximum(a, b_)
            a, b_ = jnp.exp2(a - most), jnp.exp2(b_ - most)
            span = pl.ds(j * HD, HD)
            joined = oall[r, mine, span, here].astype(F32) * a
            joined = (joined + oin[r, span, here].astype(F32) * b_) / (a + b_)
            att[b * size : (b + 1) * size, j * HD : (j + 1) * HD] = joined.T.astype(BF16)

    part = size // 2
    width = xall.shape[3]

    def units(b, half, first, second, count):
        return xall.at[half, pl.ds(first * SIDE + second, count), pl.ds(b * part, part)]

    def compute(blocks, xx, zz):
        span = pl.ds(pl.multiple_of((zz * SIDE + xx) * width, width), width)
        from_row, to_row = blocks[0] * size, (blocks[-1] + 1) * size
        got = jnp.dot(
            att[from_row:to_row, :], wv[:, span], preferred_element_type=F32
        ).astype(BF16)
        for k, b in enumerate(blocks):
            here = pl.ds(b * part, part)
            xall[0, xx * SIDE + zz, here] = got[k * size : k * size + part]
            xall[1, zz * SIDE + xx, here] = got[k * size + part : (k + 1) * size]

    def out_push(b, half, sem, src, dst, target):
        s = 2 * b + half
        remote(src, dst, br_s.at[s], br_r.at[5 * s + sem], target).start()

    def out_arrived(b, half, sem, block):
        s = 2 * b + half
        arrived(block, br_s.at[s], br_r.at[5 * s + sem])

    def first(blocks):
        loop(SIDE, lambda k: compute(blocks, around(x_, 2), around(z, k)))
        loop(SIDE - 1, lambda k: compute(blocks, around(x_, skip_two(k)), around(z, 2)))
        for b in blocks:
            for half in range(2):
                c, to, back = spot[half], *ahead[half]
                out_push(b, half, 0, units(b, half, around(c, 2), 0, 2), bl1.at[b, half], to)
                out_push(b, half, 1, units(b, half, around(c, 2), 2, 2), br1.at[b, half], back)
        loop(
            9,
            lambda k: compute(
                blocks, around(x_, skip_two(k // 3)), around(z, skip_two(lax.rem(k, 3)))
            ),
        )
        for b in blocks:
            for half in range(2):
                c, to, back = spot[half], *ahead[half]
                out_push(b, half, 2, units(b, half, around(c, 1), 2, 2), bl2.at[b, half, hi], to)
                out_push(b, half, 3, units(b, half, around(c, -1), 0, 2), br2.at[b, half, lo], back)

    def second(b):
        for half in range(2):
            c = spot[half]
            out_arrived(b, half, 0, bl1.at[b, half])
            block = units(b, half, around(c, 1), 0, 2)
            block[...] = (block[...].astype(F32) + bl1[b, half].astype(F32)).astype(BF16)
            out_push(b, half, 2, block, bl2.at[b, half, lo], ahead[half][0])
            out_arrived(b, half, 1, br1.at[b, half])
            block = units(b, half, around(c, -1), 2, 2)
            block[...] = (block[...].astype(F32) + br1[b, half].astype(F32)).astype(BF16)
            out_push(b, half, 3, block, br2.at[b, half, hi], ahead[half][1])

    def third(b):
        for half in range(2):
            c = spot[half]
            out_arrived(b, half, 2, bl2.at[b, half])
            out_arrived(b, half, 3, br2.at[b, half])
            block = units(b, half, c, 0, SIDE)
            total = block[...].astype(F32) + bl2[b, half].astype(F32) + br2[b, half].astype(F32)
            block[...] = total.astype(BF16)
            for k in (1, 3, 2, 0):
                other = around(spot[1 - half], k)
                target = (after, other * SIDE + x_) if half == 0 else (after, z * SIDE + other)
                src = xall.at[half, c * SIDE + other, pl.ds(b * part, part)]
                out_push(b, half, 4, src, bz2.at[b, half, k], target)

    results = []

    def fourth(b):
        if b > 1:
            results[b - 2].wait()
        for half in range(2):
            out_arrived(b, half, 4, bz2.at[b, half])
            total = bz2[b, half, 0].astype(F32)
            for k in range(1, SIDE):
                total += bz2[b, half, k].astype(F32)
            outv[b % 2, pl.ds(half * part, part), :] = total
        to = out.at[pl.ds(b * size, size)]
        results.append(pltpu.make_async_copy(outv.at[b % 2], to, loc.at[10 + b]))
        results[b].start()

    computed(0)
    for g in range(GROUPS):
        passages_wait(g)
        stored(0, g)
    finish(0)
    for half in range(2):
        gone = xall.at[half, pl.ds(0, N_DEV - 1)]
        remote(gone, gone, ag_s.at[half], ag_r.at[0], right).wait_send()
    loads[9].wait()
    for group in FIRSTS:
        for b in group:
            join(b)
        first(group)
    computed(1)
    stored(1, 0)
    second(0)
    second(1)
    for g in range(1, GROUPS):
        stored(1, g)
    finish(1)
    pl.semaphore_wait(ready, 1)
    third(0)
    join(2)
    first((2,))
    third(1)
    join(3)
    first((3,))
    second(2)
    second(3)
    third(2)
    third(3)
    for b in range(BLOCKS):
        fourth(b)
    for copy in sends:
        copy.wait_send()

    def gone(block, sem):
        remote(block, block, sem, br_r.at[0], right).wait_send()

    for half in range(2):
        gone(parts[half].at[pl.ds(0, SIDE - 1)], rs_s.at[2 * half])
        gone(parts[half].at[0, pl.ds(0, SIDE - 1)], rs_s.at[2 * half + 1])
        for b in range(BLOCKS):
            gone(units(b, half, 0, 0, N_DEV), br_s.at[2 * b + half])
    for g in range(GROUPS):
        gone(sent[g].at[pl.ds(0, N_DEV - 1)], st_s.at[g])
    for copy in results[-2:]:
        copy.wait()


def layer(home, retrieved, order, x, hid, kvw, qw, ow, store, rec, freq):
    anywhere = pl.BlockSpec(memory_space=pl.ANY)
    vmem = pl.BlockSpec(memory_space=pltpu.VMEM)
    smem = pl.BlockSpec(memory_space=pltpu.SMEM)
    dma = pltpu.SemaphoreType.DMA
    d_here = x.shape[1]
    cols = 4 * QLEN
    part = REQ_SECTION * QLEN // BLOCKS // 2
    width = ow.shape[1] // N_DEV
    assert width == d_here

    def bf16(*shape):
        return pltpu.VMEM(shape, BF16)

    def f32(*shape):
        return pltpu.VMEM(shape, F32)

    return pl.pallas_call(
        layer_kernel,
        out_shape=jax.ShapeDtypeStruct((REQ_SECTION * QLEN, width), F32),
        in_specs=[smem] * 3 + [anywhere] * 6 + [vmem] * 2,
        out_specs=anywhere,
        scratch_shapes=[
            pltpu.SMEM((SLOTS,), jnp.int32),
            bf16(2, N_DEV, QLEN, d_here),
            bf16(*qw.shape),
            bf16(*kvw.shape),
            bf16(REQ_SECTION, GROUP, d_here),
            bf16(SIDE, SIDE, GROUP, HD),
            bf16(SIDE, SIDE, GROUP, HD),
            bf16(2, 2, GROUP, HD),
            bf16(2, 2, GROUP, HD),
            bf16(2, SIDE, GROUP, HD),
            bf16(2, SIDE, GROUP, HD),
            bf16(2, GROUP, HD),
            bf16(2, 2, GROUP, HD),
            f32(2, QLEN, 2 * HD),
            bf16(*store.shape),
            *[bf16(N_DEV, CAP, piece, 2 * HD) for piece in PIECES],
            *[bf16(N_DEV * CAP, piece, 2 * HD) for piece in PIECES],
            bf16(REQ_SECTION, 4, QLEN, HD),
            bf16(REQ_SECTION, FROWS, HD),
            bf16(REQ_SECTION, FROWS, HD),
            bf16(QLEN, HD),
            bf16(QLEN, HD),
            f32(REQ_SECTION, HD, cols),
            f32(REQ_SECTION, 1, cols),
            f32(REQ_SECTION, 1, cols),
            f32(GROUP, HD),
            bf16(REQ_SECTION, 2, 2 * HD, QLEN),
            f32(REQ_SECTION, 2, 8, QLEN),
            bf16(REQ_SECTION, 2 * HD, QLEN),
            f32(REQ_SECTION, 8, QLEN),
            bf16(*ow.shape),
            bf16(REQ_SECTION * QLEN, 2 * HD),
            bf16(BLOCKS, 2, 2, part, width),
            bf16(BLOCKS, 2, 2, part, width),
            bf16(BLOCKS, 2, SIDE, part, width),
            bf16(BLOCKS, 2, SIDE, part, width),
            bf16(BLOCKS, 2, SIDE, part, width),
            f32(2, 2 * part, width),
            dma((10 + BLOCKS,)),
            dma((GROUPS,)),
            dma((2,)),
            dma((30,)),
            dma((4,)),
            dma((16,)),
            dma((GROUPS,)),
            dma((GROUPS,)),
            dma((2,)),
            dma((2,)),
            dma((2 + BLOCKS,)),
            dma((2 + BLOCKS,)),
            dma((2 * BLOCKS,)),
            dma((10 * BLOCKS,)),
            pltpu.SemaphoreType.REGULAR,
        ],
        compiler_params=pltpu.CompilerParams(
            collective_id=0, has_side_effects=True, vmem_limit_bytes=63 * 2**20
        ),
        name="layer",
    )(home, retrieved, order, x, hid, kvw, qw, ow, store, rec, freq)


def body(
    activations, q_weight, out_weight, kv_weight, passage_store,
    passage_home, retrieved, slot_order, recomputed, passage_hidden,
):
    exponents = -np.arange(HD // 2, dtype=np.float32) * np.float32(2.0 / HD)
    frequency = np.float32(ROPE_BASE) ** exponents
    frequency = jnp.asarray(np.concatenate([frequency, frequency])[None])
    hidden = passage_hidden[0].transpose(1, 0, 2).reshape(RECOMP * SLOTS, -1)
    out = layer(
        passage_home, retrieved, slot_order, activations[0], hidden, kv_weight[0], q_weight[0],
        out_weight[0], passage_store[0], recomputed, frequency,
    )
    return out.astype(BF16)[None]


def solution(mesh):
    in_specs = (
        P("section", None, "dev"),
        P("section", None, "dev"),
        P("section", "dev", None),
        P("section", "dev", None),
        P("section", "dev", None, None, None),
        P("section", None),
        P("section", None, None),
        P("section", None, None),
        P("section", None, None),
        P("section", None, None, "dev"),
    )
    out_specs = P("section", None, "dev")
    return jax.shard_map(body, mesh=mesh, in_specs=in_specs, out_specs=out_specs, check_vma=False)
```

```python
import functools

import jax
import jax.numpy as jnp
import numpy as np
from jax import lax
from jax.experimental import pallas as pl
from jax.experimental.pallas import tpu as pltpu
from jax.sharding import PartitionSpec as P

QH = 32
KVH = 8
HD = 128
PASS_LEN = 512
TOPK = 8
RECOMP = 77
REQ_SECTION = 2
QLEN = 256
SLOTS = 16
CAP = 2
PASS_DEV = 4
SIDE = 4
N_DEV = 16
FRESH = 39
GROUP = QLEN + FRESH * SLOTS
FROWS = 320
KEPT = PASS_LEN - RECOMP
HALF = 224
PIECES = (128, 64, 32)
STARTS = (0, 128, 192)
GROUPS = len(PIECES)
BLOCKS = 4
FIRSTS = ((0,), (1,))
ROPE_BASE = 500000.0
MESH = pl.DeviceIdType.MESH
F32 = jnp.float32
BF16 = jnp.bfloat16
SCALE = HD**-0.5 * 1.4426950408889634


def lane_tables(angles):
    sign = jnp.where(lax.broadcasted_iota(jnp.int32, (1, HD), 1) < HD // 2, -1.0, 1.0)
    return jnp.cos(angles), jnp.sin(angles) * sign


def turned(v, cosine, sine):
    return v * cosine + pltpu.roll(v, HD // 2, axis=1) * sine


def place():
    d = lax.axis_index("dev")
    return lax.axis_index("section"), d // SIDE, lax.rem(d, SIDE)


def around(v, step):
    return lax.rem(v + step + SIDE, SIDE)


def remote(src, dst, send, recv, target):
    return pltpu.make_async_remote_copy(
        src_ref=src,
        dst_ref=dst,
        send_sem=send,
        recv_sem=recv,
        device_id=target,
        device_id_type=MESH,
    )


STEPS = (
    (1, 1), (3, 3), (0, 2), (1, 3), (3, 1), (2, 0), (2, 1), (0, 3),
    (3, 2), (1, 0), (2, 3), (0, 1), (1, 2), (3, 0), (2, 2),
)


def layer_kernel(
    home, retrieved, order, x, hid, kvw, qw, ow, store, rec, freq, out,
    ent, xall, qv, kvv, rows, pa, pb, l1, r1, l2, r2, z1, z2, qacc,
    storev, out0, out1, out2, st0, st1, st2, q4, kf, vf, ko, vo, acc, m, l,
    angle, oall, lall, oin, lin, wv, att, bl1, br1, bl2, br2, bz2, outv,
    loc, own_s, ag_s, ag_r, rs_s, rs_r, st_s, st_r, q_s, q_r, ex_s, ex_r, br_s, br_r, ready,
):
    sec = lax.axis_index("section")
    me = lax.axis_index("dev")
    z, x_ = me // SIDE, lax.rem(me, SIDE)
    sections = lax.axis_size("section")
    after, before = lax.rem(sec + 1, sections), lax.rem(sec + sections - 1, sections)
    mine = lax.rem(me, 2)

    def at(zz, xx):
        return (sec, zz * SIDE + xx)

    right, left = at(z, around(x_, 1)), at(z, around(x_, -1))
    down, up = at(around(z, 1), x_), at(around(z, -1), x_)
    pair = (sec, me + 1 - 2 * mine)
    ahead = [(right, left), (down, up)]
    spot = [x_, z]

    greeted = [right, left, down, up, (after, me), (before, me)]
    barrier = pltpu.get_barrier_semaphore()
    for target in greeted:
        pl.semaphore_signal(barrier, inc=1, device_id=target, device_id_type=MESH)

    first_rows, last_rows = FRESH * SLOTS, (RECOMP - FRESH) * SLOTS
    loads = [
        pltpu.make_async_copy(kvw, kvv, loc.at[0]),
        pltpu.make_async_copy(x.at[pl.ds(0, QLEN)], rows.at[0, pl.ds(0, QLEN)], loc.at[1]),
        pltpu.make_async_copy(x.at[pl.ds(QLEN, QLEN)], rows.at[1, pl.ds(0, QLEN)], loc.at[2]),
        pltpu.make_async_copy(
            hid.at[pl.ds(0, first_rows)], rows.at[0, pl.ds(QLEN, first_rows)], loc.at[3]
        ),
        pltpu.make_async_copy(
            hid.at[pl.ds(first_rows, last_rows)], rows.at[1, pl.ds(QLEN, last_rows)], loc.at[4]
        ),
        pltpu.make_async_copy(store, storev, loc.at[5]),
        pltpu.make_async_copy(qw, qv, loc.at[6]),
        pltpu.make_async_copy(x.at[pl.ds(0, QLEN)], xall.at[0, me], loc.at[7]),
        pltpu.make_async_copy(x.at[pl.ds(QLEN, QLEN)], xall.at[1, me], loc.at[8]),
        pltpu.make_async_copy(ow, wv, loc.at[9]),
    ]
    for load in loads:
        load.start()
    rest = rows.at[1, pl.ds(QLEN + last_rows, GROUP - QLEN - last_rows)]
    rest[...] = jnp.zeros_like(rest)
    pl.semaphore_wait(barrier, len(greeted))

    def chunk(half, first, second):
        if half == 0:
            return around(z, second) * SIDE + around(x_, first)
        return around(z, first) * SIDE + around(x_, second)

    top, bottom = pl.ds(0, QLEN // 2), pl.ds(QLEN // 2, QLEN // 2)
    whole = pl.ds(0, QLEN)
    sends = []

    def ag(half, src, span, sem, target, own=False):
        to = xall.at[half, src, span]
        frm = x.at[pl.ds(half * QLEN, QLEN)] if own else to
        remote(frm, to, ag_s.at[half], ag_r.at[15 * half + sem], target).start()

    def ag_wait(half, src, sem):
        to = xall.at[half, src, whole]
        remote(to, to, ag_s.at[half], ag_r.at[15 * half + sem], right).wait_recv()

    for half in range(2):
        ag(half, me, whole, 0, ahead[half][0], True)
        ag(half, me, whole, 1, ahead[half][1], True)
    for half in range(2):
        ag(half, me, whole, 3, ahead[1 - half][0], True)
        ag(half, me, whole, 4, ahead[1 - half][1], True)

    def push(group, src, dst, send, recv, target):
        copy = remote(src, dst, send, recv, target)
        copy.start()
        group.append(copy)

    def arrived(block, send, recv):
        remote(block, block, send, recv, right).wait_recv()

    def project(xx, zz):
        head = 2 * zz + xx // 2
        span = pl.ds(pl.multiple_of(head * 2 * HD, 2 * HD), 2 * HD)
        part = jnp.dot(rows[lax.rem(xx, 2)], kvv[:, span], preferred_element_type=F32)
        part = part.astype(BF16)
        pa[xx, zz] = part[:, :HD]
        pb[zz, xx] = part[:, HD:]

    def loop(count, step):
        def one(k, carry):
            step(k)
            return carry

        lax.fori_loop(0, count, one, 0)

    def skip_two(t):
        return t + t // 2

    parts = [pa, pb]
    lo, hi = pl.ds(0, 2), pl.ds(2, 2)

    def rs(half, src, dst, sem, target):
        remote(src, dst, rs_s.at[2 * half + sem // 4], rs_r.at[8 * half + sem], target).start()

    def rs_arrived(half, block, sem):
        arrived(block, rs_s.at[2 * half + sem // 4], rs_r.at[8 * half + sem])

    upper, lower = pl.ds(0, GROUP // 32 * 16), pl.ds(GROUP // 32 * 16, GROUP - GROUP // 32 * 16)

    def rs_first(half):
        p, c = parts[half], spot[half]
        rs(half, p.at[around(c, 2), lo], l1.at[half], 0, ahead[half][0])
        rs(half, p.at[around(c, 2), hi], r1.at[half], 1, ahead[half][1])

    for k in range(5):
        loads[k].wait()
    loop(SIDE, lambda k: project(around(x_, 2), around(z, k)))
    rs_first(0)
    loop(SIDE - 1, lambda k: project(around(x_, skip_two(k)), around(z, 2)))
    rs_first(1)
    loop(9, lambda k: project(around(x_, skip_two(k // 3)), around(z, skip_two(lax.rem(k, 3)))))

    for half in range(2):
        src = chunk(half, -1, 0)
        ag_wait(half, src, 0)
        ag(half, src, top, 2, ahead[half][0])
        ag(half, src, whole, 6, ahead[1 - half][0])
        ag(half, src, whole, 7, ahead[1 - half][1])
        src = chunk(half, 1, 0)
        ag_wait(half, src, 1)
        ag(half, src, bottom, 2, ahead[half][1])
        ag(half, src, whole, 9, ahead[1 - half][0])
        ag(half, src, whole, 10, ahead[1 - half][1])
    for half in range(2):
        p, c = parts[half], spot[half]
        rs(half, p.at[around(c, 1), hi], l2.at[half, hi], 2, ahead[half][0])
        rs(half, p.at[around(c, -1), lo], r2.at[half, lo], 3, ahead[half][1])

    homes = [home[0, retrieved[0, j // TOPK, j % TOPK]] for j in range(SLOTS)]
    owners = [h // PASS_DEV for h in homes]
    entries = []
    for j in range(SLOTS):
        rank = jnp.int32(0)
        for i in range(j):
            rank = rank + jnp.where(owners[i] == owners[j], 1, 0)
        entries.append(owners[j] * CAP + rank)
        ent[j] = entries[j]
    frequency = freq[...]
    sent, st = [out0, out1, out2], [st0, st1, st2]
    loads[5].wait()
    for c in range(CAP):
        row, slot, offset = jnp.int32(0), jnp.int32(0), jnp.int32(0)
        for j in range(SLOTS):
            hit = entries[j] == me * CAP + c
            row = jnp.where(hit, lax.rem(homes[j], PASS_DEV), row)
            slot = jnp.where(hit, j, slot)
            offset = jnp.where(hit, order[0, j // TOPK, j % TOPK] * PASS_LEN, offset)
        dropped = rec[0, pl.ds(slot, 1), :]
        ahead_of = (dropped - lax.broadcasted_iota(jnp.int32, (1, RECOMP), 1)).astype(F32)
        index = lax.broadcasted_iota(jnp.int32, (2 * HALF, RECOMP), 0).astype(F32)
        count = jnp.sum(jnp.where(ahead_of <= index, 1.0, 0.0), axis=1, keepdims=True)
        keep = index[:, :1] + count
        lanes = lax.broadcasted_iota(jnp.int32, (2 * HALF, PASS_LEN), 1).astype(F32)
        pick = jnp.where(lanes == keep, 1.0, 0.0).astype(BF16)
        cosine, sine = lane_tables(frequency * offset.astype(F32))

        def one_head(h):
            kept = jnp.dot(pick, storev[row, h], preferred_element_type=F32)
            keys = turned(kept[:, :HD], cosine, sine).astype(BF16)
            values = kept[:, HD:].astype(BF16)
            for half in range(2):
                for g in range(GROUPS):
                    start = half * HALF + STARTS[g]
                    to = sent[g].at[2 * h + half, c]
                    to[:, :HD] = keys[start : start + PIECES[g]]
                    to[:, HD:] = values[start : start + PIECES[g]]

        loop(KVH, one_head)

    for g in range(GROUPS):
        copy = pltpu.make_async_copy(
            sent[g].at[me], st[g].at[pl.ds(2 * me, CAP)], own_s.at[g]
        )
        copy.start()

    def passages(g):
        for dz, dx in STEPS:
            other = around(z, dz) * SIDE + around(x_, dx)
            to = st[g].at[pl.ds(2 * me, CAP)]
            remote(sent[g].at[other], to, st_s.at[g], st_r.at[g], (sec, other)).start()

    def passages_wait(g):
        pltpu.make_async_copy(
            sent[g].at[me], st[g].at[pl.ds(2 * me, CAP)], own_s.at[g]
        ).wait()
        arrived(st[g].at[pl.ds(0, CAP * (N_DEV - 1))], st_s.at[g], st_r.at[g])

    for half in range(2):
        src = chunk(half, 2, 0)
        ag_wait(half, src, 2)
        ag(half, src, whole, 12, ahead[1 - half][0])
        ag(half, src, whole, 13, ahead[1 - half][1])

    def second_axis(k, first):
        b = 3 + 3 * k
        for half in range(2):
            src = chunk(half, first, -1)
            ag_wait(half, src, b)
            ag(half, src, top, b + 2, ahead[1 - half][0])
            src = chunk(half, first, 1)
            ag_wait(half, src, b + 1)
            ag(half, src, bottom, b + 2, ahead[1 - half][1])

    second_axis(0, 0)

    for half in range(2):
        p, c = parts[half], spot[half]
        rs_arrived(half, l1.at[half], 0)
        block = p.at[around(c, 1), lo]
        block[...] = (block[...].astype(F32) + l1[half].astype(F32)).astype(BF16)
        rs(half, block, l2.at[half, lo], 2, ahead[half][0])
        rs_arrived(half, r1.at[half], 1)
        block = p.at[around(c, -1), hi]
        block[...] = (block[...].astype(F32) + r1[half].astype(F32)).astype(BF16)
        rs(half, block, r2.at[half, hi], 3, ahead[half][1])

    second_axis(1, -1)
    second_axis(2, 1)
    second_axis(3, 2)

    for half in range(2):
        p, c = parts[half], spot[half]
        rs_arrived(half, l2.at[half], 2)
        rs_arrived(half, r2.at[half], 3)
        for u in range(SIDE):
            block = p.at[c, u]
            total = block[...].astype(F32) + l2[half, u].astype(F32) + r2[half, u].astype(F32)
            block[...] = total.astype(BF16)
        far = around(spot[1 - half], 2)
        rs(half, p.at[c, far, upper], z1.at[half, upper], 4, ahead[1 - half][0])
        rs(half, p.at[c, far, lower], z1.at[half, lower], 5, ahead[1 - half][1])

    for k in (6, 7, 8):
        loads[k].wait()
    for half in range(2):
        for k in range(SIDE):
            ag_wait(half, chunk(half, (0, -1, 1, 2)[k], 2), 5 + 3 * k)
    pl.semaphore_signal(ready, inc=1, device_id=(before, me), device_id_type=MESH)
    passages(0)

    def project_queries(k):
        span = pl.ds(pl.multiple_of(k * 2 * QLEN, 2 * QLEN), 2 * QLEN)
        weight = qv[span, :]
        for half in range(2):
            qacc[half] += jnp.dot(xall[half, k], weight, preferred_element_type=F32)

    qacc[...] = jnp.zeros_like(qacc)
    loop(N_DEV, project_queries)
    token_at = lax.broadcasted_iota(jnp.int32, (QLEN, 1), 0) + TOPK * PASS_LEN
    token_angles = token_at.astype(F32) * frequency
    cosine, sine = lane_tables(token_angles)
    base = 2 * mine
    for half in range(2):
        for j in range(2):
            head = turned(qacc[half, :, j * HD : (j + 1) * HD], cosine, sine)
            q4[half, base + j] = head.astype(BF16)

    def share_queries(r):
        block = q4.at[r, pl.ds(base, 2)]
        push(sends, block, block, q_s.at[r], q_r.at[r], pair)

    share_queries(0)

    for half in range(2):
        p, c, d = parts[half], spot[half], spot[1 - half]
        for k, span in ((1, upper), (-1, lower)):
            rs_arrived(half, z1.at[half, span], 4 + (1 - k) // 2)
            block = p.at[c, around(d, k), span]
            block[...] = (block[...].astype(F32) + z1[half, span].astype(F32)).astype(BF16)
        rs(half, p.at[c, around(d, 1)], z2.at[half, 0], 6, ahead[1 - half][0])
        rs(half, p.at[c, around(d, -1)], z2.at[half, 1], 7, ahead[1 - half][1])
    for g in range(1, GROUPS):
        passages(g)
    share_queries(1)

    slot_at = lax.broadcasted_iota(jnp.int32, (SLOTS, 1), 0)
    offsets = jnp.zeros((SLOTS, 1), jnp.int32)
    for j in range(SLOTS):
        offsets = jnp.where(slot_at == j, order[0, j // TOPK, j % TOPK] * PASS_LEN, offsets)
    places = rec[0] + offsets
    angle[pl.ds(0, QLEN)] = token_angles
    for i in range(FRESH):
        here = places[:, i : i + 1]
        if FRESH + i < RECOMP:
            here = jnp.where(mine == 0, here, places[:, FRESH + i : FRESH + i + 1])
        angle[pl.ds(QLEN + i * SLOTS, SLOTS)] = here.astype(F32) * frequency
    cosine, sine = lane_tables(angle[...])
    for half in range(2):
        p, c = parts[half], spot[half]
        total = p[c, spot[1 - half]].astype(F32)
        for k in range(2):
            rs_arrived(half, z2.at[half, k], 6 + k)
            total += z2[half, k].astype(F32)
        total = total.astype(BF16).astype(F32)
        if half == 0:
            total = turned(total, cosine, sine)
        own_to, fresh_to = (ko, kf) if half == 0 else (vo, vf)
        own_to[...] = total[:QLEN].astype(BF16)
        fresh = total[QLEN:].reshape(FRESH, SLOTS, HD)
        for r in range(REQ_SECTION):
            rows_of = fresh[:, r * TOPK : (r + 1) * TOPK].reshape(FRESH * TOPK, HD)
            filler = jnp.zeros((FROWS - FRESH * TOPK, HD), F32)
            fresh_to[r] = jnp.concatenate([rows_of, filler], axis=0).astype(BF16)

    cols = 4 * QLEN

    def score(keys, queries):
        s = lax.dot_general(
            keys, queries, (((1,), (1,)), ((), ())), preferred_element_type=F32
        )
        return s * SCALE

    def update(r, scores, values):
        old = m[r]
        new = old
        for s in scores:
            new = jnp.maximum(new, jnp.max(s, axis=0, keepdims=True))
        scale = jnp.exp2(old - new)
        total, mixed = l[r] * scale, acc[r] * scale
        for s, v in zip(scores, values):
            weights = jnp.exp2(s - new)
            total = total + jnp.sum(weights, axis=0, keepdims=True)
            mixed = mixed + lax.dot_general(
                v, weights.astype(BF16), (((0,), (0,)), ((), ())), preferred_element_type=F32
            )
        m[r], l[r], acc[r] = new, total, mixed

    def bias(count, valid):
        index = lax.broadcasted_iota(jnp.int32, (count, 1), 0)
        return jnp.where(index < valid, 0.0, -jnp.inf)

    def queries_of(r):
        return q4[r].reshape(cols, HD)

    def stored(r, g):
        many = 2 if g == 0 else 4

        def some(k):
            scores, values = [], []
            for i in range(many):
                e = ent[r * TOPK + many * k + i]
                block = st[g].at[e]
                s = score(block[:, :HD], queries_of(r))
                if g == GROUPS - 1:
                    s = s + bias(PIECES[g], PIECES[g] - (2 * HALF - KEPT) * mine)
                scores.append(s)
                values.append(block[:, HD:])
            update(r, scores, values)

        loop(TOPK // many, some)

    def computed(r):
        block = q4.at[r, pl.ds(2 - base, 2)]
        arrived(block, q_s.at[r], q_r.at[r])
        s = score(kf[r], queries_of(r)) + bias(FROWS, FRESH * TOPK - TOPK * mine)
        update(r, [s], [vf[r]])

        @pl.when(mine == r)
        def _():
            s = score(ko[...], queries_of(r))
            keys_at = lax.broadcasted_iota(jnp.int32, (QLEN, cols), 0)
            query_at = lax.rem(lax.broadcasted_iota(jnp.int32, (QLEN, cols), 1), QLEN)
            s = jnp.where(keys_at <= query_at, s, -jnp.inf)
            update(r, [s], [vo[...]])

    m[...] = jnp.full_like(m, -1e30)
    l[...] = jnp.zeros_like(l)
    acc[...] = jnp.zeros_like(acc)
    per = BLOCKS // REQ_SECTION

    size = REQ_SECTION * QLEN // BLOCKS

    def finish(r):
        done = (acc[r] / l[r]).astype(BF16)
        level = m[r] + jnp.log2(l[r])
        for j in range(4):
            span = slice(j * QLEN, (j + 1) * QLEN)
            oall[r, j // 2, pl.ds((j % 2) * HD, HD), :] = done[:, span]
            lall[r, j // 2, pl.ds(j % 2, 1), :] = level[:, span]
        sem = (1 + per) * r
        push(sends, lall.at[r, 1 - mine], lin.at[r], ex_s.at[sem], ex_r.at[sem], pair)
        for k in range(per):
            span = pl.ds(k * size, size)
            push(sends, oall.at[r, 1 - mine, :, span], oin.at[r, :, span],
                 ex_s.at[sem + 1 + k], ex_r.at[sem + 1 + k], pair)

    def join(b):
        r, k = b // per, b % per
        sem = (1 + per) * r
        if k == 0:
            arrived(lin.at[r], ex_s.at[sem], ex_r.at[sem])
        here = pl.ds(k * size, size)
        arrived(oin.at[r, :, here], ex_s.at[sem + 1 + k], ex_r.at[sem + 1 + k])
        for j in range(2):
            a, b_ = lall[r, mine, pl.ds(j, 1), here], lin[r, pl.ds(j, 1), here]
            most = jnp.maximum(a, b_)
            a, b_ = jnp.exp2(a - most), jnp.exp2(b_ - most)
            span = pl.ds(j * HD, HD)
            joined = oall[r, mine, span, here].astype(F32) * a
            joined = (joined + oin[r, span, here].astype(F32) * b_) / (a + b_)
            att[b * size : (b + 1) * size, j * HD : (j + 1) * HD] = joined.T.astype(BF16)

    part = size // 2
    width = xall.shape[3]

    def units(b, half, first, second, count):
        return xall.at[half, pl.ds(first * SIDE + second, count), pl.ds(b * part, part)]

    def compute(blocks, xx, zz):
        span = pl.ds(pl.multiple_of((zz * SIDE + xx) * width, width), width)
        from_row, to_row = blocks[0] * size, (blocks[-1] + 1) * size
        got = jnp.dot(
            att[from_row:to_row, :], wv[:, span], preferred_element_type=F32
        ).astype(BF16)
        for k, b in enumerate(blocks):
            here = pl.ds(b * part, part)
            xall[0, xx * SIDE + zz, here] = got[k * size : k * size + part]
            xall[1, zz * SIDE + xx, here] = got[k * size + part : (k + 1) * size]

    def out_push(b, half, sem, src, dst, target):
        s = 2 * b + half
        remote(src, dst, br_s.at[s], br_r.at[5 * s + sem], target).start()

    def out_arrived(b, half, sem, block):
        s = 2 * b + half
        arrived(block, br_s.at[s], br_r.at[5 * s + sem])

    def first(blocks):
        loop(SIDE, lambda k: compute(blocks, around(x_, 2), around(z, k)))
        loop(SIDE - 1, lambda k: compute(blocks, around(x_, skip_two(k)), around(z, 2)))
        for b in blocks:
            for half in range(2):
                c, to, back = spot[half], *ahead[half]
                out_push(b, half, 0, units(b, half, around(c, 2), 0, 2), bl1.at[b, half], to)
                out_push(b, half, 1, units(b, half, around(c, 2), 2, 2), br1.at[b, half], back)
        loop(
            9,
            lambda k: compute(
                blocks, around(x_, skip_two(k // 3)), around(z, skip_two(lax.rem(k, 3)))
            ),
        )
        for b in blocks:
            for half in range(2):
                c, to, back = spot[half], *ahead[half]
                out_push(b, half, 2, units(b, half, around(c, 1), 2, 2), bl2.at[b, half, hi], to)
                out_push(b, half, 3, units(b, half, around(c, -1), 0, 2), br2.at[b, half, lo], back)

    def second(b):
        for half in range(2):
            c = spot[half]
            out_arrived(b, half, 0, bl1.at[b, half])
            block = units(b, half, around(c, 1), 0, 2)
            block[...] = (block[...].astype(F32) + bl1[b, half].astype(F32)).astype(BF16)
            out_push(b, half, 2, block, bl2.at[b, half, lo], ahead[half][0])
            out_arrived(b, half, 1, br1.at[b, half])
            block = units(b, half, around(c, -1), 2, 2)
            block[...] = (block[...].astype(F32) + br1[b, half].astype(F32)).astype(BF16)
            out_push(b, half, 3, block, br2.at[b, half, hi], ahead[half][1])

    def third(b):
        for half in range(2):
            c = spot[half]
            out_arrived(b, half, 2, bl2.at[b, half])
            out_arrived(b, half, 3, br2.at[b, half])
            block = units(b, half, c, 0, SIDE)
            total = block[...].astype(F32) + bl2[b, half].astype(F32) + br2[b, half].astype(F32)
            block[...] = total.astype(BF16)
            for k in (1, 3, 2, 0):
                other = around(spot[1 - half], k)
                target = (after, other * SIDE + x_) if half == 0 else (after, z * SIDE + other)
                src = xall.at[half, c * SIDE + other, pl.ds(b * part, part)]
                out_push(b, half, 4, src, bz2.at[b, half, k], target)

    results = []

    def fourth(b):
        if b > 1:
            results[b - 2].wait()
        for half in range(2):
            out_arrived(b, half, 4, bz2.at[b, half])
            total = bz2[b, half, 0].astype(F32)
            for k in range(1, SIDE):
                total += bz2[b, half, k].astype(F32)
            outv[b % 2, pl.ds(half * part, part), :] = total
        to = out.at[pl.ds(b * size, size)]
        results.append(pltpu.make_async_copy(outv.at[b % 2], to, loc.at[10 + b]))
        results[b].start()

    computed(0)
    for g in range(GROUPS):
        passages_wait(g)
        stored(0, g)
    finish(0)
    for half in range(2):
        gone = xall.at[half, pl.ds(0, N_DEV - 1)]
        remote(gone, gone, ag_s.at[half], ag_r.at[0], right).wait_send()
    loads[9].wait()
    for group in FIRSTS:
        for b in group:
            join(b)
        first(group)
    computed(1)
    stored(1, 0)
    second(0)
    second(1)
    for g in range(1, GROUPS):
        stored(1, g)
    finish(1)
    pl.semaphore_wait(ready, 1)
    third(0)
    join(2)
    first((2,))
    third(1)
    join(3)
    first((3,))
    second(2)
    second(3)
    third(2)
    third(3)
    for b in range(BLOCKS):
        fourth(b)
    for copy in sends:
        copy.wait_send()

    def gone(block, sem):
        remote(block, block, sem, br_r.at[0], right).wait_send()

    for half in range(2):
        gone(parts[half].at[pl.ds(0, SIDE - 1)], rs_s.at[2 * half])
        gone(parts[half].at[0, pl.ds(0, SIDE - 1)], rs_s.at[2 * half + 1])
        for b in range(BLOCKS):
            gone(units(b, half, 0, 0, N_DEV), br_s.at[2 * b + half])
    for g in range(GROUPS):
        gone(sent[g].at[pl.ds(0, N_DEV - 1)], st_s.at[g])
    for copy in results[-2:]:
        copy.wait()


def layer(home, retrieved, order, x, hid, kvw, qw, ow, store, rec, freq):
    anywhere = pl.BlockSpec(memory_space=pl.ANY)
    vmem = pl.BlockSpec(memory_space=pltpu.VMEM)
    smem = pl.BlockSpec(memory_space=pltpu.SMEM)
    dma = pltpu.SemaphoreType.DMA
    d_here = x.shape[1]
    cols = 4 * QLEN
    part = REQ_SECTION * QLEN // BLOCKS // 2
    width = ow.shape[1] // N_DEV
    assert width == d_here

    def bf16(*shape):
        return pltpu.VMEM(shape, BF16)

    def f32(*shape):
        return pltpu.VMEM(shape, F32)

    return pl.pallas_call(
        layer_kernel,
        out_shape=jax.ShapeDtypeStruct((REQ_SECTION * QLEN, width), F32),
        in_specs=[smem] * 3 + [anywhere] * 6 + [vmem] * 2,
        out_specs=anywhere,
        scratch_shapes=[
            pltpu.SMEM((SLOTS,), jnp.int32),
            bf16(2, N_DEV, QLEN, d_here),
            bf16(*qw.shape),
            bf16(*kvw.shape),
            bf16(REQ_SECTION, GROUP, d_here),
            bf16(SIDE, SIDE, GROUP, HD),
            bf16(SIDE, SIDE, GROUP, HD),
            bf16(2, 2, GROUP, HD),
            bf16(2, 2, GROUP, HD),
            bf16(2, SIDE, GROUP, HD),
            bf16(2, SIDE, GROUP, HD),
            bf16(2, GROUP, HD),
            bf16(2, 2, GROUP, HD),
            f32(2, QLEN, 2 * HD),
            bf16(*store.shape),
            *[bf16(N_DEV, CAP, piece, 2 * HD) for piece in PIECES],
            *[bf16(N_DEV * CAP, piece, 2 * HD) for piece in PIECES],
            bf16(REQ_SECTION, 4, QLEN, HD),
            bf16(REQ_SECTION, FROWS, HD),
            bf16(REQ_SECTION, FROWS, HD),
            bf16(QLEN, HD),
            bf16(QLEN, HD),
            f32(REQ_SECTION, HD, cols),
            f32(REQ_SECTION, 1, cols),
            f32(REQ_SECTION, 1, cols),
            f32(GROUP, HD),
            bf16(REQ_SECTION, 2, 2 * HD, QLEN),
            f32(REQ_SECTION, 2, 8, QLEN),
            bf16(REQ_SECTION, 2 * HD, QLEN),
            f32(REQ_SECTION, 8, QLEN),
            bf16(*ow.shape),
            bf16(REQ_SECTION * QLEN, 2 * HD),
            bf16(BLOCKS, 2, 2, part, width),
            bf16(BLOCKS, 2, 2, part, width),
            bf16(BLOCKS, 2, SIDE, part, width),
            bf16(BLOCKS, 2, SIDE, part, width),
            bf16(BLOCKS, 2, SIDE, part, width),
            f32(2, 2 * part, width),
            dma((10 + BLOCKS,)),
            dma((GROUPS,)),
            dma((2,)),
            dma((30,)),
            dma((4,)),
            dma((16,)),
            dma((GROUPS,)),
            dma((GROUPS,)),
            dma((2,)),
            dma((2,)),
            dma((2 + BLOCKS,)),
            dma((2 + BLOCKS,)),
            dma((2 * BLOCKS,)),
            dma((10 * BLOCKS,)),
            pltpu.SemaphoreType.REGULAR,
        ],
        compiler_params=pltpu.CompilerParams(
            collective_id=0, has_side_effects=True, vmem_limit_bytes=63 * 2**20
        ),
        name="layer",
    )(home, retrieved, order, x, hid, kvw, qw, ow, store, rec, freq)


def body(
    activations, q_weight, out_weight, kv_weight, passage_store,
    passage_home, retrieved, slot_order, recomputed, passage_hidden,
):
    exponents = -np.arange(HD // 2, dtype=np.float32) * np.float32(2.0 / HD)
    frequency = np.float32(ROPE_BASE) ** exponents
    frequency = jnp.asarray(np.concatenate([frequency, frequency])[None])
    hidden = passage_hidden[0].transpose(1, 0, 2).reshape(RECOMP * SLOTS, -1)
    out = layer(
        passage_home, retrieved, slot_order, activations[0], hidden, kv_weight[0], q_weight[0],
        out_weight[0], passage_store[0], recomputed, frequency,
    )
    return out.astype(BF16)[None]


def solution(mesh):
    in_specs = (
        P("section", None, "dev"),
        P("section", None, "dev"),
        P("section", "dev", None),
        P("section", "dev", None),
        P("section", "dev", None, None, None),
        P("section", None),
        P("section", None, None),
        P("section", None, None),
        P("section", None, None),
        P("section", None, None, "dev"),
    )
    out_specs = P("section", None, "dev")
    return jax.shard_map(body, mesh=mesh, in_specs=in_specs, out_specs=out_specs, check_vma=False)
```
